32 devices in a mesh: exc: 2 (over core), line: 16 (over z, y, x).
Axes of the slice: x: 2, y: 2, z: 4, core: 2. Of those that a mesh axis runs over, the one named last changes fastest.
Arguments:
- adj_e: float32 [3, 2, 1024, 1024], P(None, 'exc', 'line'), parts along dimension 1, may hold values from -6 to 6
- adj_h: float32 [3, 2, 1024, 1024], P(None, 'exc', 'line'), parts along dimension 1, may hold values from -6 to 6
- fwd_e: bfloat16 [2, 3, 2, 1024, 1024], P(None, None, 'exc', 'line'), parts along dimension 2, may hold values from -6 to 6
- permittivity: float32 [1, 1024, 1024], P(None, 'line'), may hold values from 1 to 6
- design_mask: int32 [1, 1024, 1024], P(None, 'line'), may hold values 0 or 1
- inverse: bfloat16 [1024, 1024], replicated, may hold values from -0.03125 to 0.6875
- omega: float32 [2], P('exc'), parts along dimension 0, may hold values from 0.3 to 2.5
- port_mode: float32 [2048], P('exc'), parts along dimension 0, may hold values from -6 to 6
- port_plane: int32 [2], P('exc'), parts along dimension 0, may hold values from 0 to 1023
Outputs:
- adj_e_out: float32 [3, 2, 1024, 1024], P(None, 'exc', 'line'), parts along dimension 1
- adj_h_out: float32 [3, 2, 1024, 1024], P(None, 'exc', 'line'), parts along dimension 1
- gradient: float32 [2, 1024, 1024], P('exc', 'line'), parts along dimension 0
The draws below stay inside these ranges and needn't reach their ends.
There are 2 independent parts, one for each index of `exc`. The reference program is written for one: setup_inputs(seed, part) draws one part's arguments, and reference() takes and returns one part's arrays. A program takes and returns all parts, laid end to end along the dimension named above; an argument that names none is the same for every part. Nothing has to cross between parts.
All inputs are finite; a program needn't handle non-finite values. No bound on the sum of `design_mask` on one device may be relied on, other than what follows from the above.
Results may differ from the reference program's by a relative error of at most 0.005.
Values may be sent and summed in bfloat16 or wider, within the bound.
A program may use at most 64 MiB of HBM per device.

```python
import math
import jax
import jax.numpy as jnp
from jax import lax

CELLS = 1024
PLANES = 1
STEPS = 2


def draw_inverse(key, part):
    diag_key, off_key = jax.random.split(key)
    diagonal = jax.random.uniform(diag_key, (CELLS,), jnp.float32, 0.5, 0.6875)
    spread = jax.random.uniform(off_key, (CELLS, CELLS), jnp.float32, -0.03125, 0.03125)
    identity = jnp.arange(CELLS)[:, None] == jnp.arange(CELLS)[None, :]
    return jnp.where(identity, diagonal[None, :], spread).astype(jnp.bfloat16)


def set_ends(drawn, key, least, top_value):
    extent = drawn.shape
    place = [jax.random.randint(jax.random.fold_in(key, axis), (), 0, extent[axis]) for axis in range(len(extent))]
    drawn = drawn.at[tuple(place)].set(least)
    longest = extent.index(max(extent))
    place[longest] = (place[longest] + 1) % extent[longest]
    return drawn.at[tuple(place)].set(top_value)


def block_scale(rng, extent, shards, least, largest):
    level, own = 1.0, jax.random.fold_in(rng, 6)
    for dim, blocks in shards:
        heights = jnp.exp(jax.random.uniform(jax.random.fold_in(own, dim), (blocks,), jnp.float32, least / len(shards), largest / len(shards)))
        level = level * jnp.repeat(heights, extent[dim] // blocks).reshape([-1 if axis == dim else 1 for axis in range(len(extent))])
    return level


def normal_values(own_key, dims, width, bound, cuts=(), kind=jnp.bfloat16):
    entries = jax.random.normal(own_key, dims, jnp.float32) * width
    if len(cuts) > 0:
        entries = block_scale(own_key, dims, cuts, -0.22, 0.18) * entries
    return jnp.clip(entries, min=-bound, max=bound).astype(kind)


def setup_inputs(seed: int = 0, part: int = 0) -> dict:
    arg_keys = jax.random.split(jax.random.key(seed), 10)
    part_splits = jax.random.split(jax.random.fold_in(arg_keys[9], part), 10)
    return {
        "adj_e": normal_values(part_splits[0], (3, PLANES, CELLS, CELLS), 1.0, 6.0, ((2, 16),), jnp.float32),
        "adj_h": normal_values(part_splits[1], (3, PLANES, CELLS, CELLS), 1.0, 6.0, ((2, 16),), jnp.float32),
        "fwd_e": normal_values(part_splits[2], (STEPS, 3, PLANES, CELLS, CELLS), 1.0, 6.0, ((3, 16),)),
        "permittivity": jnp.clip(jnp.exp(math.log(6.0) - 1.7917595 * jax.random.uniform(arg_keys[3], (PLANES, CELLS, CELLS), jnp.float32) ** block_scale(arg_keys[3], (PLANES, CELLS, CELLS), ((1, 16),), -0.2, 0.2)), 1.0, 6.0),
        "design_mask": set_ends((jax.random.randint(arg_keys[4], (PLANES, CELLS, CELLS), 0, 2) < 1).astype(jnp.int32), jax.random.fold_in(arg_keys[4], 1), 0, 1),
        "inverse": draw_inverse(jax.random.fold_in(arg_keys[9], 71), part),
        "omega": jnp.clip(jnp.exp(jax.random.uniform(part_splits[6], (1,), jnp.float32, math.log(0.3), math.log(2.5))), 0.3, 2.5),
        "port_mode": normal_values(part_splits[7], (CELLS,), 1.0, 6.0, (), jnp.float32),
        "port_plane": jax.random.randint(part_splits[8], (1,), 0, CELLS).astype(jnp.int32),
    }


COURANT = 0.4


def lower_diff(padded, along):
    inner = padded.shape[along] - 2
    middle = lax.slice_in_dim(padded, 1, inner + 1, axis=along)
    return middle - lax.slice_in_dim(padded, 0, inner, axis=along)


def upper_diff(padded, along):
    inner = padded.shape[along] - 2
    middle = lax.slice_in_dim(padded, 1, inner + 1, axis=along)
    return lax.slice_in_dim(padded, 2, inner + 2, axis=along) - middle


def zero_rim(stacked, along):
    widths = [(0, 0)] * stacked.ndim
    widths[along] = (1, 1)
    return jnp.pad(stacked, widths)


def curl_along_y(fields, inverse_eps, extend, along):
    electric_x, electric_y, electric_z = fields[0], fields[1], fields[2]
    magnetic_x, magnetic_y, magnetic_z = fields[3], fields[4], fields[5]
    scaled = COURANT * inverse_eps
    lower_terms = lower_diff(extend(jnp.stack([magnetic_x, magnetic_z]), along), along)
    electric_x = electric_x + scaled * lower_terms[1]
    electric_z = electric_z - scaled * lower_terms[0]
    upper_terms = upper_diff(extend(jnp.stack([electric_x, electric_z]), along), along)
    magnetic_x = magnetic_x - COURANT * upper_terms[1]
    magnetic_z = magnetic_z + COURANT * upper_terms[0]
    return jnp.stack([electric_x, electric_y, electric_z, magnetic_x, magnetic_y, magnetic_z])


def curl_along_xz(fields, inverse_eps, extend, along):
    electric_x, electric_y, electric_z = fields[0], fields[1], fields[2]
    magnetic_x, magnetic_y, magnetic_z = fields[3], fields[4], fields[5]
    scaled = COURANT * inverse_eps
    depth_terms = lower_diff(zero_rim(jnp.stack([magnetic_x, magnetic_y]), 1), 1)
    across = lower_diff(extend(jnp.stack([magnetic_y, magnetic_z]), along), along)
    electric_x = electric_x - scaled * depth_terms[1]
    electric_y = electric_y + scaled * (depth_terms[0] - across[1])
    electric_z = electric_z + scaled * across[0]
    depth_upper = upper_diff(zero_rim(jnp.stack([electric_x, electric_y]), 1), 1)
    across_upper = upper_diff(extend(jnp.stack([electric_y, electric_z]), along), along)
    magnetic_x = magnetic_x + COURANT * depth_upper[1]
    magnetic_y = magnetic_y + COURANT * (across_upper[1] - depth_upper[0])
    magnetic_z = magnetic_z - COURANT * across_upper[0]
    return jnp.stack([electric_x, electric_y, electric_z, magnetic_x, magnetic_y, magnetic_z])


def line_solve(rounded, inverse):
    flattened = rounded.reshape(-1, rounded.shape[-1])
    solved = lax.dot_general(flattened, inverse, (((1,), (1,)), ((), ())), preferred_element_type=jnp.float32)
    return solved.reshape(rounded.shape)


def reference(adj_e, adj_h, fwd_e, permittivity, design_mask, inverse, omega, port_mode, port_plane):
    fields = jnp.concatenate([adj_e, adj_h], 0)
    inverse_rows = 1.0 / permittivity
    inverse_cols = jnp.swapaxes(inverse_rows, 1, 2)
    frequency = omega[0]
    profile = port_mode
    column = (jnp.arange(CELLS, dtype=jnp.int32) == port_plane[0]).astype(jnp.float32)
    mask_weight = design_mask.astype(jnp.float32)
    gradient = jnp.zeros((PLANES, CELLS, CELLS), jnp.float32)
    for instant in range(STEPS):
        amplitude = jnp.cos(frequency * (instant + 1))
        fields = fields.at[2].add((amplitude * profile[None, :, None]) * column[None, None, :])
        fields = curl_along_y(fields, inverse_rows, zero_rim, 2)
        fields = line_solve(fields.astype(jnp.bfloat16), inverse)
        fields = curl_along_xz(fields, inverse_rows, zero_rim, 3)
        turned = jnp.swapaxes(fields.astype(jnp.bfloat16), 2, 3)
        fields = line_solve(turned, inverse)
        snapshot = fwd_e[instant].astype(jnp.float32)
        intersection = fields[0] * snapshot[0] + fields[1] * snapshot[1] + fields[2] * snapshot[2]
        gradient = gradient + mask_weight * intersection * (inverse_cols * inverse_cols)
        if instant + 1 < STEPS:
            fields = jnp.swapaxes(fields, 2, 3)
    return fields[:3], fields[3:], gradient
```

```python
import functools

import jax
import jax.numpy as jnp
from jax import lax
from jax.experimental import pallas as pl
from jax.experimental.pallas import tpu as pltpu
from jax.sharding import PartitionSpec as P

COURANT = 0.4


def extended(array, sides, width):
    for axis, dim in sides:
        devices, length = (lax.axis_size(axis), array.shape[dim])
        up = [(i, (i + 1) % devices) for i in range(devices - 1)]
        down = [(j, i) for i, j in up]
        last = lax.slice_in_dim(array, length - width, length, axis=dim)
        first = lax.slice_in_dim(array, 0, width, axis=dim)
        before = lax.ppermute(last, axis, up)
        after = lax.ppermute(first, axis, down)
        array = jnp.concatenate([before, array, after], axis=dim)
    return array


def lower_diff(padded, along):
    inner = padded.shape[along] - 2
    middle = lax.slice_in_dim(padded, 1, inner + 1, axis=along)
    return middle - lax.slice_in_dim(padded, 0, inner, axis=along)


def upper_diff(padded, along):
    inner = padded.shape[along] - 2
    middle = lax.slice_in_dim(padded, 1, inner + 1, axis=along)
    return lax.slice_in_dim(padded, 2, inner + 2, axis=along) - middle


def zero_rim(stacked, along):
    widths = [(0, 0)] * stacked.ndim
    widths[along] = (1, 1)
    return jnp.pad(stacked, widths)


def row_rim(stacked, along):
    return extended(stacked, (("line", 2),), 1)


def column_rim(stacked, along):
    return extended(stacked, (("line", 2),), 1)


def curl_along_y(fields, inverse_eps, extend, along):
    electric_x, electric_y, electric_z = (fields[0], fields[1], fields[2])
    magnetic_x, magnetic_y, magnetic_z = (fields[3], fields[4], fields[5])
    scaled = COURANT * inverse_eps
    lower_terms = lower_diff(extend(jnp.stack([magnetic_x, magnetic_z]), along), along)
    electric_x = electric_x + scaled * lower_terms[1]
    electric_z = electric_z - scaled * lower_terms[0]
    upper_terms = upper_diff(extend(jnp.stack([electric_x, electric_z]), along), along)
    magnetic_x = magnetic_x - COURANT * upper_terms[1]
    magnetic_z = magnetic_z + COURANT * upper_terms[0]
    return jnp.stack([electric_x, electric_y, electric_z, magnetic_x, magnetic_y, magnetic_z])


def curl_along_xz(fields, inverse_eps, extend, along):
    electric_x, electric_y, electric_z = (fields[0], fields[1], fields[2])
    magnetic_x, magnetic_y, magnetic_z = (fields[3], fields[4], fields[5])
    scaled = COURANT * inverse_eps
    depth_terms = lower_diff(zero_rim(jnp.stack([magnetic_x, magnetic_y]), 1), 1)
    across = lower_diff(extend(jnp.stack([magnetic_y, magnetic_z]), along), along)
    electric_x = electric_x - scaled * depth_terms[1]
    electric_y = electric_y + scaled * (depth_terms[0] - across[1])
    electric_z = electric_z + scaled * across[0]
    depth_upper = upper_diff(zero_rim(jnp.stack([electric_x, electric_y]), 1), 1)
    across_upper = upper_diff(extend(jnp.stack([electric_y, electric_z]), along), along)
    magnetic_x = magnetic_x + COURANT * depth_upper[1]
    magnetic_y = magnetic_y + COURANT * (across_upper[1] - depth_upper[0])
    magnetic_z = magnetic_z - COURANT * across_upper[0]
    return jnp.stack([electric_x, electric_y, electric_z, magnetic_x, magnetic_y, magnetic_z])


def line_solve(rounded, inverse):
    flattened = rounded.reshape(-1, rounded.shape[-1])
    solved = lax.dot_general(
        flattened, inverse, (((1,), (1,)), ((), ())), preferred_element_type=jnp.float32
    )
    return solved.reshape(rounded.shape)


def fold_lines(field, line_count):
    strip_width = field.shape[-2]
    block = field.shape[-1] // line_count
    regrouped = field.reshape(field.shape[:-2] + (strip_width, line_count, block))
    regrouped = jnp.moveaxis(regrouped, -3, -1)
    return regrouped.reshape(field.shape[:-2] + (line_count, block * strip_width))


def unfold(received, block):
    line_count = received.shape[-2]
    strip_width = received.shape[-1] // block
    regrouped = received.reshape(received.shape[:-2] + (line_count, block, strip_width))
    regrouped = jnp.moveaxis(regrouped, -3, -2)
    return regrouped.reshape(received.shape[:-2] + (block, line_count * strip_width))


def accumulate(gradient, fields, snapshot, mask_weight, inverse_cols):
    forward = snapshot.astype(jnp.float32)
    intersection = fields[0] * forward[0] + fields[1] * forward[1] + fields[2] * forward[2]
    return gradient + mask_weight * intersection * (inverse_cols * inverse_cols)


def plain_per_device(
    adj_e, adj_h, fwd_e, permittivity, design_mask, inverse, omega, port_mode, port_plane
):
    line_cells = inverse.shape[0]
    strip_width = adj_e.shape[2]
    step_count = fwd_e.shape[0]
    line_count = lax.axis_size("line")
    fields = jnp.concatenate([adj_e, adj_h], 0)
    inverse_rows = 1.0 / permittivity
    eps_turned = lax.all_to_all(
        fold_lines(permittivity, line_count), "line", split_axis=1, concat_axis=1, tiled=True
    )
    inverse_cols = 1.0 / unfold(eps_turned, strip_width)
    frequency = omega[0]
    plane_at = port_plane[0]
    offset = lax.axis_index("line") * strip_width
    column = (jnp.arange(line_cells, dtype=jnp.int32) == plane_at).astype(jnp.float32)
    profile_rows = lax.dynamic_slice_in_dim(port_mode, offset, strip_width)
    mask_weight = design_mask.astype(jnp.float32)
    gradient = jnp.zeros(permittivity.shape, jnp.float32)
    for instant in range(step_count):
        amplitude = jnp.cos(frequency * (instant + 1))
        fields = fields.at[2].add(amplitude * profile_rows[None, :, None] * column[None, None, :])
        fields = curl_along_y(fields, inverse_rows, row_rim, 2)
        fields = line_solve(fields.astype(jnp.bfloat16), inverse)
        turned = unfold(
            lax.all_to_all(
                fold_lines(fields, line_count), "line", split_axis=2, concat_axis=2, tiled=True
            ),
            strip_width,
        )
        turned = curl_along_xz(turned, inverse_cols, column_rim, 2)
        turned = line_solve(turned.astype(jnp.bfloat16), inverse)
        gradient = accumulate(gradient, turned, fwd_e[instant], mask_weight, inverse_cols)
        if instant + 1 < step_count:
            fields = unfold(
                lax.all_to_all(
                    fold_lines(turned, line_count), "line", split_axis=2, concat_axis=2, tiled=True
                ),
                strip_width,
            )
    return (turned[:3], turned[3:], gradient)


LANES = 128
MESH = pl.DeviceIdType.MESH
PAD = 8
F32, BF16 = (jnp.float32, jnp.bfloat16)
PAIRS_X = ((0, 1), (2, 3), (4, 5))
PAIRS_Y = ((0, 2), (1, 4), (5, 3))


def contract(left, right):
    return lax.dot_general(left, right, (((1,), (1,)), ((), ())), preferred_element_type=F32)


def shifted_down(value, first):
    row = lax.broadcasted_iota(jnp.int32, value.shape, 0)
    return jnp.where(row == 0, first, pltpu.roll(value, 1, 0))


def shifted_up(value, last):
    rows = value.shape[0]
    row = lax.broadcasted_iota(jnp.int32, value.shape, 0)
    return jnp.where(row == rows - 1, last, pltpu.roll(value, rows - 1, 0))


def kernel(
    n, e_hbm, h_hbm, fwd_hbm, perm_hbm, mask_hbm, inv_hbm, omega, mode, plane,
    oe, oh, og,
    e, h, fwd, perm, mask, inv, halo, halo_lo, halo_hi, p_send, p_recv, eps_t, r_first, r_second, inv_eps,
    mode_col, lines, solved, send, recv, grad,
    load_sem, halo_send_sem, halo_recv_sem, p_send_sem, p_recv_sem, send_sem, recv_sem,
):
    me = lax.axis_index("line")
    strip = perm.shape[0]
    cells = inv.shape[0]
    above, below = (lax.rem(me + 1, n), lax.rem(me + n - 1, n))

    barrier = pltpu.get_barrier_semaphore()

    def greet(k, carry):
        pl.semaphore_signal(barrier, inc=1, device_id={"line": lax.rem(me + k, n)}, device_id_type=MESH)
        return carry

    lax.fori_loop(1, n, greet, 0)

    loads = []
    for source, target in (
        (perm_hbm.at[0], perm), (e_hbm.at[:, 0], e), (h_hbm.at[:, 0], h), (inv_hbm, inv),
        (fwd_hbm.at[:, :, 0], fwd), (mask_hbm.at[0], mask),
    ):
        copy = pltpu.make_async_copy(source, target, load_sem.at[len(loads)])
        copy.start()
        loads.append(copy)

    lane = lax.broadcasted_iota(jnp.int32, (1, LANES), 1)
    low = lane < strip

    for block in range(cells // LANES):
        line = jnp.broadcast_to(mode[block : block + 1, :], (LANES, LANES))
        mode_col[block * LANES : (block + 1) * LANES, :] = line.T
    mode_col[cells:, :] = jnp.zeros((PAD, LANES), F32)
    amplitudes = [jnp.cos(jnp.full((1, LANES), omega[0] * (s + 1), F32)) for s in range(2)]
    at_plane = plane[0]

    loads[0].wait()
    twice = jnp.concatenate([perm[...], perm[...]], 0)
    eps_t[...] = twice.T
    for block in range(n):
        first = eps_t[block * strip : block * strip + strip // 2, :]
        second = eps_t[block * strip + strip // 2 : (block + 1) * strip, :]
        p_send[block] = jnp.where(low, first, second)
    r_first[0:cells, :] = COURANT * (1.0 / eps_t[...])
    r_first[cells:, :] = jnp.zeros((PAD, LANES), F32)

    loads[1].wait()
    loads[2].wait()
    halo[...] = jnp.concatenate(
        [
            e[0, 0:1, :], e[2, 0:1, :], h[0, 0:1, :], h[2, 0:1, :], perm[0:1, :],
            h[0, strip - 1 : strip, :], h[2, strip - 1 : strip, :], perm[0:1, :],
        ],
        0,
    )

    pl.semaphore_wait(barrier, n - 1)

    to_above = pltpu.make_async_remote_copy(
        halo, halo_lo, halo_send_sem.at[0], halo_recv_sem.at[0], device_id={"line": above}, device_id_type=MESH
    )
    to_below = pltpu.make_async_remote_copy(
        halo, halo_hi, halo_send_sem.at[1], halo_recv_sem.at[1], device_id={"line": below}, device_id_type=MESH
    )
    to_above.start()
    to_below.start()

    def p_copy(to, slot):
        return pltpu.make_async_remote_copy(
            p_send.at[to], p_recv.at[slot], p_send_sem.at[to], p_recv_sem.at[slot],
            device_id={"line": to}, device_id_type=MESH,
        )

    def p_start(k, carry):
        p_copy(lax.rem(me + k, n), me).start()
        return carry

    lax.fori_loop(1, n, p_start, 0)
    p_recv[me] = p_send[me]

    to_above.wait()
    to_below.wait()
    is_first, is_last = (me == 0, me == n - 1)
    x_at = lax.broadcasted_iota(jnp.int32, (1, cells), 1)
    column = jnp.where(x_at == at_plane, 1.0, 0.0)
    profile = mode_col[pl.ds(pl.multiple_of(me * strip, strip), strip + PAD), :] * amplitudes[0]
    profile = jnp.concatenate([profile] * (cells // LANES), 1)
    source = profile * column
    r = COURANT * (1.0 / perm[...])
    ex, ez, hx, hz = (e[0], e[2] + source[0:strip], h[0], h[2])
    hx_lo = jnp.where(is_first, 0.0, halo_lo[5:6, :])
    hz_lo = jnp.where(is_first, 0.0, halo_lo[6:7, :])
    ex = ex + r * (hz - shifted_down(hz, hz_lo))
    ez = ez - r * (hx - shifted_down(hx, hx_lo))
    r_hi = COURANT * (1.0 / halo_hi[4:5, :])
    ex_hi = halo_hi[0:1, :] + r_hi * (halo_hi[3:4, :] - hz[strip - 1 : strip])
    ez_hi = halo_hi[1:2, :] + source[strip : strip + 1] - r_hi * (halo_hi[2:3, :] - hx[strip - 1 : strip])
    ex_hi = jnp.where(is_last, 0.0, ex_hi)
    ez_hi = jnp.where(is_last, 0.0, ez_hi)
    hx = hx - COURANT * (shifted_up(ez, ez_hi) - ez)
    hz = hz + COURANT * (shifted_up(ex, ex_hi) - ex)
    for at, value in enumerate((ex, e[1], ez, hx, h[1], hz)):
        lines[at * strip : (at + 1) * strip, :] = value.astype(BF16)
    loads[3].wait()

    def copy_out(stage, to, slot):
        return pltpu.make_async_remote_copy(
            send.at[stage, to], recv.at[stage, slot], send_sem.at[stage, to], recv_sem.at[stage, slot],
            device_id={"line": to}, device_id_type=MESH,
        )

    def send_all(stage):
        def go(k, carry):
            copy_out(stage, lax.rem(me + k, n), me).start()
            return carry

        lax.fori_loop(1, n, go, 0)
        recv[stage, me] = send[stage, me]

    def receive_all(stage):
        def take(k, carry):
            other = lax.rem(me + k, n)
            copy_out(stage, other, other).wait_recv()
            return carry

        lax.fori_loop(1, n, take, 0)

    def solve_turned():
        for pair in range(3):
            solved[pair, 0:PAD, :] = jnp.zeros((PAD, LANES), F32)
            solved[pair, cells + PAD :, :] = jnp.zeros((PAD, LANES), F32)
        result = contract(inv[...], lines[...])
        for pair in range(3):
            solved[pair, PAD : cells + PAD, :] = result[:, pair * LANES : (pair + 1) * LANES]

    def assemble(stage, pairs, order):
        half = n // 2
        for k in range(half):
            for pair, (one, two) in enumerate(pairs):
                a, b = (recv[stage, 2 * k, pair], recv[stage, 2 * k + 1, pair])
                at_one, at_two = (order.index(one) * strip, order.index(two) * strip)
                cut = slice(k * LANES, (k + 1) * LANES)
                lines[at_one : at_one + strip, cut] = jnp.concatenate([a[:, :strip], b[:, :strip]], 1)
                lines[at_two : at_two + strip, cut] = jnp.concatenate([a[:, strip:], b[:, strip:]], 1)

    rows = LANES

    def put(stage, start, tiles):
        for pair, tile in enumerate(tiles):
            for part in range(rows // strip):
                send[stage, start // strip + part, pair] = tile[part * strip : (part + 1) * strip].astype(BF16)

    def extended(pair, start, back):
        return solved[pair, start + PAD - back : start + PAD - back + rows + PAD, :]

    def curl_x(stage):
        for start in range(0, cells, rows):
            row = lax.broadcasted_iota(jnp.int32, (rows + PAD, LANES), 0) + start
            p, q, t = (extended(0, start, 0), extended(1, start, 0), extended(2, start, 0))
            r = r_first[start : start + rows + PAD, :]
            dt = t - extended(2, start, 1)
            p = p + r * jnp.where(low, -t, q - dt)
            q = q + jnp.where(low, r * dt, -COURANT * p)
            s = jnp.where(row < cells, jnp.where(low, q, p), 0.0)
            ds = (pltpu.roll(s, rows + PAD - 1, 0) - s)[0:rows]
            p, q, t = (p[0:rows], q[0:rows], t[0:rows])
            t = t + jnp.where(low, COURANT * (ds + p), -COURANT * ds)
            put(stage, start, (p, q, t))

    def curl_y(stage):
        here = jnp.where(low, 0.0, 1.0) * jnp.where(lane - strip + me * strip == at_plane, 1.0, 0.0)
        for start in range(0, cells, rows):
            row = lax.broadcasted_iota(jnp.int32, (rows + PAD, LANES), 0) + start
            p, t = (extended(0, start, 0), extended(2, start, 0))
            r = r_second[start : start + rows + PAD, :]
            p = p + (amplitudes[1] * mode_col[start : start + rows + PAD, :]) * here
            dt = t - extended(2, start, 1)
            p = p + jnp.where(low, r, -r) * dt
            p = jnp.where(row < cells, p, 0.0)
            dp = (pltpu.roll(p, rows + PAD - 1, 0) - p)[0:rows]
            t = t[0:rows] + jnp.where(low, COURANT, -COURANT) * dp
            put(stage, start, (p[0:rows], extended(1, start, 0)[0:rows], t))

    def along(electric, instant):
        return (
            electric[0] * fwd[instant, 0].astype(F32)
            + electric[1] * fwd[instant, 1].astype(F32)
            + electric[2] * fwd[instant, 2].astype(F32)
        )

    solve_turned()
    curl_x(0)
    send_all(0)

    def p_take(k, carry):
        other = lax.rem(me + k, n)
        p_copy(other, other).wait_recv()
        return carry

    lax.fori_loop(1, n, p_take, 0)
    for k in range(n // 2):
        a, b = (p_recv[2 * k], p_recv[2 * k + 1])
        cut = slice(k * LANES, (k + 1) * LANES)
        inv_eps[0 : strip // 2, cut] = 1.0 / jnp.concatenate([a[:, :strip], b[:, :strip]], 1)
        inv_eps[strip // 2 :, cut] = 1.0 / jnp.concatenate([a[:, strip:], b[:, strip:]], 1)
    both = jnp.concatenate([inv_eps[...], inv_eps[...]], 0)
    r_second[0:cells, :] = COURANT * both.T
    r_second[cells:, :] = jnp.zeros((PAD, LANES), F32)
    loads[4].wait()
    loads[5].wait()
    weight = mask[...].astype(F32)

    receive_all(0)
    assemble(0, PAIRS_X, (0, 2, 1, 4, 5, 3))
    solve_turned()
    curl_y(1)
    send_all(1)

    square = inv_eps[...] * inv_eps[...]
    electric = contract(lines[0 : 3 * strip, :], inv[...])
    parts = (electric[0:strip], electric[2 * strip :], electric[strip : 2 * strip])
    grad[...] = weight * along(parts, 0) * square

    receive_all(1)
    assemble(1, PAIRS_Y, (0, 1, 2, 3, 4, 5))
    solve_turned()
    curl_x(2)
    send_all(2)

    receive_all(2)
    assemble(2, PAIRS_X, (0, 1, 2, 3, 4, 5))
    final = contract(lines[...], inv[...])
    parts = [final[at * strip : (at + 1) * strip] for at in range(6)]
    for at in range(3):
        oe[at, 0] = parts[at]
        oh[at, 0] = parts[3 + at]
    og[0] = grad[...] + weight * along(parts, 1) * square

    def settle(k, carry):
        other = lax.rem(me + k, n)
        p_copy(other, other).wait_send()
        for stage in range(3):
            copy_out(stage, other, other).wait_send()
        return carry

    lax.fori_loop(1, n, settle, 0)


def fused(adj_e, adj_h, fwd_e, permittivity, design_mask, inverse, omega, port_mode, port_plane):
    n = lax.axis_size("line")
    cells, strip = (inverse.shape[0], adj_e.shape[2])
    steps = fwd_e.shape[0]
    anywhere = pl.BlockSpec(memory_space=pl.ANY)
    vmem = pl.BlockSpec(memory_space=pltpu.VMEM)
    smem = pl.BlockSpec(memory_space=pltpu.SMEM)
    scratch = [
        pltpu.VMEM((3, strip, cells), F32),
        pltpu.VMEM((3, strip, cells), F32),
        pltpu.VMEM((steps, 3, strip, cells), BF16),
        pltpu.VMEM((strip, cells), F32),
        pltpu.VMEM((strip, cells), jnp.int32),
        pltpu.VMEM((cells, cells), BF16),
        pltpu.VMEM((8, cells), F32),
        pltpu.VMEM((8, cells), F32),
        pltpu.VMEM((8, cells), F32),
        pltpu.VMEM((n, strip // 2, LANES), F32),
        pltpu.VMEM((n, strip // 2, LANES), F32),
        pltpu.VMEM((cells, LANES), F32),
        pltpu.VMEM((cells + PAD, LANES), F32),
        pltpu.VMEM((cells + PAD, LANES), F32),
        pltpu.VMEM((strip, cells), F32),
        pltpu.VMEM((cells + PAD, LANES), F32),
        pltpu.VMEM((6 * strip, cells), BF16),
        pltpu.VMEM((3, cells + 2 * PAD, LANES), F32),
        pltpu.VMEM((3, n, 3, strip, LANES), BF16),
        pltpu.VMEM((3, n, 3, strip, LANES), BF16),
        pltpu.VMEM((strip, cells), F32),
        pltpu.SemaphoreType.DMA((6,)),
        pltpu.SemaphoreType.DMA((2,)),
        pltpu.SemaphoreType.DMA((2,)),
        pltpu.SemaphoreType.DMA((n,)),
        pltpu.SemaphoreType.DMA((n,)),
        pltpu.SemaphoreType.DMA((3, n)),
        pltpu.SemaphoreType.DMA((3, n)),
    ]
    return pl.pallas_call(
        functools.partial(kernel, n),
        out_shape=(
            jax.ShapeDtypeStruct(adj_e.shape, F32),
            jax.ShapeDtypeStruct(adj_h.shape, F32),
            jax.ShapeDtypeStruct(permittivity.shape, F32),
        ),
        in_specs=[anywhere] * 6 + [smem, vmem, smem],
        out_specs=(vmem, vmem, vmem),
        scratch_shapes=scratch,
        compiler_params=pltpu.CompilerParams(
            collective_id=0, has_side_effects=True, vmem_limit_bytes=50 * 1024 * 1024
        ),
    )(
        adj_e, adj_h, fwd_e, permittivity, design_mask, inverse, omega,
        port_mode.reshape(cells // LANES, LANES), port_plane,
    )


def per_device(adj_e, adj_h, fwd_e, permittivity, design_mask, inverse, omega, port_mode, port_plane):
    args = (adj_e, adj_h, fwd_e, permittivity, design_mask, inverse, omega, port_mode, port_plane)
    paired = 2 * adj_e.shape[2] == LANES and fwd_e.shape[0] == 2 and permittivity.shape[0] == 1
    return fused(*args) if paired else plain_per_device(*args)


def solution(mesh):
    in_specs = (
        P(None, "exc", "line", None),
        P(None, "exc", "line", None),
        P(None, None, "exc", "line", None),
        P(None, "line", None),
        P(None, "line", None),
        P(),
        P("exc"),
        P("exc"),
        P("exc"),
    )
    out_specs = (P(None, "exc", "line", None), P(None, "exc", "line", None), P("exc", "line", None))
    return jax.shard_map(
        per_device, mesh=mesh, in_specs=in_specs, out_specs=out_specs, check_vma=False
    )
```

```python
import functools

import jax
import jax.numpy as jnp
from jax import lax
from jax.experimental import pallas as pl
from jax.experimental.pallas import tpu as pltpu
from jax.sharding import PartitionSpec as P

COURANT = 0.4


def extended(array, sides, width):
    for axis, dim in sides:
        devices, length = (lax.axis_size(axis), array.shape[dim])
        up = [(i, (i + 1) % devices) for i in range(devices - 1)]
        down = [(j, i) for i, j in up]
        last = lax.slice_in_dim(array, length - width, length, axis=dim)
        first = lax.slice_in_dim(array, 0, width, axis=dim)
        before = lax.ppermute(last, axis, up)
        after = lax.ppermute(first, axis, down)
        array = jnp.concatenate([before, array, after], axis=dim)
    return array


def lower_diff(padded, along):
    inner = padded.shape[along] - 2
    middle = lax.slice_in_dim(padded, 1, inner + 1, axis=along)
    return middle - lax.slice_in_dim(padded, 0, inner, axis=along)


def upper_diff(padded, along):
    inner = padded.shape[along] - 2
    middle = lax.slice_in_dim(padded, 1, inner + 1, axis=along)
    return lax.slice_in_dim(padded, 2, inner + 2, axis=along) - middle


def zero_rim(stacked, along):
    widths = [(0, 0)] * stacked.ndim
    widths[along] = (1, 1)
    return jnp.pad(stacked, widths)


def row_rim(stacked, along):
    return extended(stacked, (("line", 2),), 1)


def column_rim(stacked, along):
    return extended(stacked, (("line", 2),), 1)


def curl_along_y(fields, inverse_eps, extend, along):
    electric_x, electric_y, electric_z = (fields[0], fields[1], fields[2])
    magnetic_x, magnetic_y, magnetic_z = (fields[3], fields[4], fields[5])
    scaled = COURANT * inverse_eps
    lower_terms = lower_diff(extend(jnp.stack([magnetic_x, magnetic_z]), along), along)
    electric_x = electric_x + scaled * lower_terms[1]
    electric_z = electric_z - scaled * lower_terms[0]
    upper_terms = upper_diff(extend(jnp.stack([electric_x, electric_z]), along), along)
    magnetic_x = magnetic_x - COURANT * upper_terms[1]
    magnetic_z = magnetic_z + COURANT * upper_terms[0]
    return jnp.stack([electric_x, electric_y, electric_z, magnetic_x, magnetic_y, magnetic_z])


def curl_along_xz(fields, inverse_eps, extend, along):
    electric_x, electric_y, electric_z = (fields[0], fields[1], fields[2])
    magnetic_x, magnetic_y, magnetic_z = (fields[3], fields[4], fields[5])
    scaled = COURANT * inverse_eps
    depth_terms = lower_diff(zero_rim(jnp.stack([magnetic_x, magnetic_y]), 1), 1)
    across = lower_diff(extend(jnp.stack([magnetic_y, magnetic_z]), along), along)
    electric_x = electric_x - scaled * depth_terms[1]
    electric_y = electric_y + scaled * (depth_terms[0] - across[1])
    electric_z = electric_z + scaled * across[0]
    depth_upper = upper_diff(zero_rim(jnp.stack([electric_x, electric_y]), 1), 1)
    across_upper = upper_diff(extend(jnp.stack([electric_y, electric_z]), along), along)
    magnetic_x = magnetic_x + COURANT * depth_upper[1]
    magnetic_y = magnetic_y + COURANT * (across_upper[1] - depth_upper[0])
    magnetic_z = magnetic_z - COURANT * across_upper[0]
    return jnp.stack([electric_x, electric_y, electric_z, magnetic_x, magnetic_y, magnetic_z])


def line_solve(rounded, inverse):
    flattened = rounded.reshape(-1, rounded.shape[-1])
    solved = lax.dot_general(
        flattened, inverse, (((1,), (1,)), ((), ())), preferred_element_type=jnp.float32
    )
    return solved.reshape(rounded.shape)


def fold_lines(field, line_count):
    strip_width = field.shape[-2]
    block = field.shape[-1] // line_count
    regrouped = field.reshape(field.shape[:-2] + (strip_width, line_count, block))
    regrouped = jnp.moveaxis(regrouped, -3, -1)
    return regrouped.reshape(field.shape[:-2] + (line_count, block * strip_width))


def unfold(received, block):
    line_count = received.shape[-2]
    strip_width = received.shape[-1] // block
    regrouped = received.reshape(received.shape[:-2] + (line_count, block, strip_width))
    regrouped = jnp.moveaxis(regrouped, -3, -2)
    return regrouped.reshape(received.shape[:-2] + (block, line_count * strip_width))


def accumulate(gradient, fields, snapshot, mask_weight, inverse_cols):
    forward = snapshot.astype(jnp.float32)
    intersection = fields[0] * forward[0] + fields[1] * forward[1] + fields[2] * forward[2]
    return gradient + mask_weight * intersection * (inverse_cols * inverse_cols)


def plain_per_device(
    adj_e, adj_h, fwd_e, permittivity, design_mask, inverse, omega, port_mode, port_plane
):
    line_cells = inverse.shape[0]
    strip_width = adj_e.shape[2]
    step_count = fwd_e.shape[0]
    line_count = lax.axis_size("line")
    fields = jnp.concatenate([adj_e, adj_h], 0)
    inverse_rows = 1.0 / permittivity
    eps_turned = lax.all_to_all(
        fold_lines(permittivity, line_count), "line", split_axis=1, concat_axis=1, tiled=True
    )
    inverse_cols = 1.0 / unfold(eps_turned, strip_width)
    frequency = omega[0]
    plane_at = port_plane[0]
    offset = lax.axis_index("line") * strip_width
    column = (jnp.arange(line_cells, dtype=jnp.int32) == plane_at).astype(jnp.float32)
    profile_rows = lax.dynamic_slice_in_dim(port_mode, offset, strip_width)
    mask_weight = design_mask.astype(jnp.float32)
    gradient = jnp.zeros(permittivity.shape, jnp.float32)
    for instant in range(step_count):
        amplitude = jnp.cos(frequency * (instant + 1))
        fields = fields.at[2].add(amplitude * profile_rows[None, :, None] * column[None, None, :])
        fields = curl_along_y(fields, inverse_rows, row_rim, 2)
        fields = line_solve(fields.astype(jnp.bfloat16), inverse)
        turned = unfold(
            lax.all_to_all(
                fold_lines(fields, line_count), "line", split_axis=2, concat_axis=2, tiled=True
            ),
            strip_width,
        )
        turned = curl_along_xz(turned, inverse_cols, column_rim, 2)
        turned = line_solve(turned.astype(jnp.bfloat16), inverse)
        gradient = accumulate(gradient, turned, fwd_e[instant], mask_weight, inverse_cols)
        if instant + 1 < step_count:
            fields = unfold(
                lax.all_to_all(
                    fold_lines(turned, line_count), "line", split_axis=2, concat_axis=2, tiled=True
                ),
                strip_width,
            )
    return (turned[:3], turned[3:], gradient)


LANES = 128
MESH = pl.DeviceIdType.MESH
PAD = 8
F32, BF16 = (jnp.float32, jnp.bfloat16)


def contract(left, right):
    return lax.dot_general(left, right, (((1,), (1,)), ((), ())), preferred_element_type=F32)


def shifted_down(value, first):
    row = lax.broadcasted_iota(jnp.int32, value.shape, 0)
    return jnp.where(row == 0, first, pltpu.roll(value, 1, 0))


def shifted_up(value, last):
    rows = value.shape[0]
    row = lax.broadcasted_iota(jnp.int32, value.shape, 0)
    return jnp.where(row == rows - 1, last, pltpu.roll(value, rows - 1, 0))


def kernel(
    n, e_hbm, h_hbm, fwd_hbm, perm_hbm, mask_hbm, inv_hbm, omega, mode_hbm, plane,
    oe, oh, og,
    e, h, fwd, perm, mask, inv, halo, halo_lo, halo_hi, p_send, p_recv, eps_t, r_first, r_second, inv_eps,
    mode_v, mode_col, lines, solved, kept, send, recv, grad,
    load_sem, halo_send_sem, halo_recv_sem, p_send_sem, p_recv_sem, send_sem, recv_sem,
):
    me = lax.axis_index("line")
    strip = perm.shape[0]
    cells = inv.shape[0]
    above, below = (lax.rem(me + 1, n), lax.rem(me + n - 1, n))

    barrier = pltpu.get_barrier_semaphore()

    def greet(k, carry):
        pl.semaphore_signal(barrier, inc=1, device_id={"line": lax.rem(me + k, n)}, device_id_type=MESH)
        return carry

    lax.fori_loop(1, n, greet, 0)

    loads = []
    for source, target in (
        (perm_hbm.at[0], perm), (mode_hbm, mode_v), (e_hbm.at[:, 0], e), (h_hbm.at[:, 0], h), (inv_hbm, inv),
        (fwd_hbm.at[:, :, 0], fwd), (mask_hbm.at[0], mask),
    ):
        copy = pltpu.make_async_copy(source, target, load_sem.at[len(loads)])
        copy.start()
        loads.append(copy)

    lane = lax.broadcasted_iota(jnp.int32, (1, LANES), 1)
    low = lane < strip

    loads[0].wait()
    twice = jnp.concatenate([perm[...], perm[...]], 0)
    eps_t[...] = twice.T
    for block in range(n):
        first = eps_t[block * strip : block * strip + strip // 2, :]
        second = eps_t[block * strip + strip // 2 : (block + 1) * strip, :]
        p_send[block] = jnp.where(low, first, second)
    r_first[0:cells, :] = COURANT * (1.0 / eps_t[...])
    r_first[cells:, :] = jnp.zeros((PAD, LANES), F32)

    loads[1].wait()
    for block in range(cells // LANES):
        line = jnp.broadcast_to(mode_v[block : block + 1, :], (LANES, LANES))
        mode_col[block * LANES : (block + 1) * LANES, :] = line.T
    mode_col[cells:, :] = jnp.zeros((PAD, LANES), F32)
    amplitudes = [jnp.cos(jnp.full((1, LANES), omega[0] * (s + 1), F32)) for s in range(2)]
    at_plane = plane[0]

    loads[2].wait()
    loads[3].wait()
    halo[...] = jnp.concatenate(
        [
            e[0, 0:1, :], e[2, 0:1, :], h[0, 0:1, :], h[2, 0:1, :], perm[0:1, :],
            h[0, strip - 1 : strip, :], h[2, strip - 1 : strip, :], perm[0:1, :],
        ],
        0,
    )

    pl.semaphore_wait(barrier, n - 1)

    to_above = pltpu.make_async_remote_copy(
        halo, halo_lo, halo_send_sem.at[0], halo_recv_sem.at[0], device_id={"line": above}, device_id_type=MESH
    )
    to_below = pltpu.make_async_remote_copy(
        halo, halo_hi, halo_send_sem.at[1], halo_recv_sem.at[1], device_id={"line": below}, device_id_type=MESH
    )
    to_above.start()
    to_below.start()

    def p_copy(to, slot):
        return pltpu.make_async_remote_copy(
            p_send.at[to], p_recv.at[slot], p_send_sem.at[to], p_recv_sem.at[slot],
            device_id={"line": to}, device_id_type=MESH,
        )

    def p_start(k, carry):
        p_copy(lax.rem(me + k, n), me).start()
        return carry

    lax.fori_loop(1, n, p_start, 0)
    p_recv[me] = p_send[me]

    to_above.wait()
    to_below.wait()
    is_first, is_last = (me == 0, me == n - 1)
    x_at = lax.broadcasted_iota(jnp.int32, (1, cells), 1)
    column = jnp.where(x_at == at_plane, 1.0, 0.0)
    profile = mode_col[pl.ds(pl.multiple_of(me * strip, strip), strip + PAD), :] * amplitudes[0]
    profile = jnp.concatenate([profile] * (cells // LANES), 1)
    source = profile * column
    r = COURANT * (1.0 / perm[...])
    ex, ez, hx, hz = (e[0], e[2] + source[0:strip], h[0], h[2])
    hx_lo = jnp.where(is_first, 0.0, halo_lo[5:6, :])
    hz_lo = jnp.where(is_first, 0.0, halo_lo[6:7, :])
    ex = ex + r * (hz - shifted_down(hz, hz_lo))
    ez = ez - r * (hx - shifted_down(hx, hx_lo))
    r_hi = COURANT * (1.0 / halo_hi[4:5, :])
    ex_hi = halo_hi[0:1, :] + r_hi * (halo_hi[3:4, :] - hz[strip - 1 : strip])
    ez_hi = halo_hi[1:2, :] + source[strip : strip + 1] - r_hi * (halo_hi[2:3, :] - hx[strip - 1 : strip])
    ex_hi = jnp.where(is_last, 0.0, ex_hi)
    ez_hi = jnp.where(is_last, 0.0, ez_hi)
    hx = hx - COURANT * (shifted_up(ez, ez_hi) - ez)
    hz = hz + COURANT * (shifted_up(ex, ex_hi) - ex)
    for at, value in enumerate((ex, ez, h[1], e[1], hz, hx)):
        lines[at * strip : (at + 1) * strip, :] = value.astype(BF16)

    def copy_out(message, to, slot):
        return pltpu.make_async_remote_copy(
            send.at[message, to], recv.at[message, slot], send_sem.at[message, to], recv_sem.at[message, slot],
            device_id={"line": to}, device_id_type=MESH,
        )

    def send_all(message):
        def go(k, carry):
            copy_out(message, lax.rem(me + k, n), me).start()
            return carry

        lax.fori_loop(1, n, go, 0)
        recv[message, me] = send[message, me]

    def receive_all(message):
        def take(k, carry):
            other = lax.rem(me + k, n)
            copy_out(message, other, other).wait_recv()
            return carry

        lax.fori_loop(1, n, take, 0)

    def assemble(message, tile):
        receive_all(message)
        at = tile * LANES
        for k in range(n // 2):
            a, b = (recv[message, 2 * k], recv[message, 2 * k + 1])
            cut = slice(k * LANES, (k + 1) * LANES)
            lines[at : at + strip, cut] = jnp.concatenate([a[:, :strip], b[:, :strip]], 1)
            lines[at + strip : at + LANES, cut] = jnp.concatenate([a[:, strip:], b[:, strip:]], 1)

    def solve_tile(tile):
        part = lines[tile * LANES : (tile + 1) * LANES, :]
        solved[tile, PAD : cells + PAD, :] = contract(inv[...], part)

    rows = LANES

    def put(message, start, tile):
        for part in range(rows // strip):
            send[message, start // strip + part] = tile[part * strip : (part + 1) * strip].astype(BF16)

    def swap(tile):
        return pltpu.roll(tile, LANES // 2, 1)

    def extended(tile, start, back):
        return solved[tile, start + PAD - back : start + PAD - back + rows + PAD, :]

    def next_row(value):
        return pltpu.roll(value, value.shape[0] - 1, 0)

    def in_grid(start):
        return lax.broadcasted_iota(jnp.int32, (rows + PAD, LANES), 0) + start < cells

    def curl_x_first(start):
        here = slice(start + PAD, start + PAD + rows)
        b, bd = (solved[1, here, :], solved[1, start + PAD - 1 : start + PAD - 1 + rows, :])
        hy, hyd = (jnp.where(low, b, swap(b)), jnp.where(low, bd, swap(bd)))
        a = solved[0, here, :] + r_first[start : start + rows, :] * jnp.where(low, -hy, hy - hyd)
        solved[0, here, :] = a
        return a

    def curl_x_second(start):
        a, b, c = (extended(0, start, 0), extended(1, start, 0), extended(2, start, 0))
        sa, sc = (swap(a), swap(c))
        dc = sc - swap(extended(2, start, 1))
        ey = b + r_first[start : start + rows + PAD, :] * (c - dc)
        ey = jnp.where(in_grid(start), ey, 0.0)
        hy = b + COURANT * ((next_row(sa) - sa) + a)
        sy = swap(ey)
        c = c - COURANT * jnp.where(low, next_row(sy) - sy, ey)
        return jnp.where(low, hy, ey)[0:rows], c[0:rows]

    def curl_y(tile, start, sign, source):
        t, td = (extended(tile, start, 0), extended(tile, start, 1))
        st, std = (swap(t), swap(td))
        p = t if source is None else t + source
        p = p + sign * r_second[start : start + rows + PAD, :] * (st - std)
        p = jnp.where(in_grid(start), p, 0.0)
        sp = swap(p)
        q = t + sign * COURANT * (next_row(sp) - sp)
        return jnp.where(low, p, q)[0:rows]

    def along(electric, instant):
        return (
            electric[0] * fwd[instant, 0].astype(F32)
            + electric[1] * fwd[instant, 1].astype(F32)
            + electric[2] * fwd[instant, 2].astype(F32)
        )

    for tile in range(3):
        solved[tile, 0:PAD, :] = jnp.zeros((PAD, LANES), F32)
        solved[tile, cells + PAD :, :] = jnp.zeros((PAD, LANES), F32)
    starts = range(0, cells, rows)

    loads[4].wait()
    result = contract(inv[...], lines[...])
    for tile in range(3):
        solved[tile, PAD : cells + PAD, :] = result[:, tile * LANES : (tile + 1) * LANES]
    for start in starts:
        curl_x_first(start)
    for start in starts:
        a = solved[0, start + PAD : start + PAD + rows, :]
        b, c = curl_x_second(start)
        put(0, start, jnp.where(low, a, swap(c)))
        put(1, start, jnp.where(low, swap(a), c))
        put(2, start, b)
    for message in range(3):
        send_all(message)

    def p_take(k, carry):
        other = lax.rem(me + k, n)
        p_copy(other, other).wait_recv()
        return carry

    lax.fori_loop(1, n, p_take, 0)
    for k in range(n // 2):
        a, b = (p_recv[2 * k], p_recv[2 * k + 1])
        cut = slice(k * LANES, (k + 1) * LANES)
        inv_eps[0 : strip // 2, cut] = 1.0 / jnp.concatenate([a[:, :strip], b[:, :strip]], 1)
        inv_eps[strip // 2 :, cut] = 1.0 / jnp.concatenate([a[:, strip:], b[:, strip:]], 1)
    both = jnp.concatenate([inv_eps[...], inv_eps[...]], 0)
    r_second[0:cells, :] = COURANT * both.T
    r_second[cells:, :] = jnp.zeros((PAD, LANES), F32)
    loads[5].wait()
    loads[6].wait()

    assemble(0, 0)
    solve_tile(0)
    for start in starts:
        kept[start : start + rows, :] = curl_y(0, start, 1.0, None)
    assemble(1, 1)
    solve_tile(1)
    here = jnp.where(low & (lane + me * strip == at_plane), 1.0, 0.0)
    for start in starts:
        source = (amplitudes[1] * mode_col[start : start + rows + PAD, :]) * here
        b = curl_y(1, start, -1.0, source)
        a = kept[start : start + rows, :]
        put(3, start, jnp.where(low, a, swap(b)))
        put(5, start, jnp.where(low, swap(a), b))
    send_all(3)
    assemble(2, 2)
    solve_tile(2)
    for start in starts:
        put(4, start, solved[2, start + PAD : start + PAD + rows, :])
    send_all(4)
    send_all(5)

    weight = mask[...].astype(F32)
    square = inv_eps[...] * inv_eps[...]
    electric = jnp.concatenate(
        [lines[0:strip, :], lines[LANES + strip * 0 : LANES + strip, :], lines[2 * LANES + strip :, :]], 0
    )
    electric = contract(electric, inv[...])
    parts = (electric[0:strip], electric[2 * strip :], electric[strip : 2 * strip])
    grad[...] = weight * along(parts, 0) * square

    for tile in range(2):
        assemble(3 + tile, tile)
        solve_tile(tile)
    for start in starts:
        put(6, start, curl_x_first(start))
    send_all(6)
    assemble(5, 2)
    solve_tile(2)
    for start in starts:
        b, c = curl_x_second(start)
        put(7, start, b)
        put(8, start, c)
    send_all(7)
    send_all(8)

    assemble(6, 0)
    pair = contract(lines[0:LANES, :], inv[...])
    oe[0, 0] = pair[:strip]
    oe[2, 0] = pair[strip:]
    assemble(7, 1)
    pair = contract(lines[LANES : 2 * LANES, :], inv[...])
    oh[1, 0] = pair[:strip]
    oe[1, 0] = pair[strip:]
    og[0] = grad[...] + weight * along((oe[0, 0], pair[strip:], oe[2, 0]), 1) * square
    assemble(8, 2)
    pair = contract(lines[2 * LANES :, :], inv[...])
    oh[2, 0] = pair[:strip]
    oh[0, 0] = pair[strip:]

    def settle(k, carry):
        other = lax.rem(me + k, n)
        p_copy(other, other).wait_send()
        for message in range(9):
            copy_out(message, other, other).wait_send()
        return carry

    lax.fori_loop(1, n, settle, 0)


def write_out(e, h, g, oe, oh, og, sem):
    copies = []
    for source, target in ((e, oe), (h, oh)):
        for at in range(3):
            copies.append(pltpu.make_async_copy(source.at[at], target.at[at], sem.at[len(copies)]))
    copies.append(pltpu.make_async_copy(g, og, sem.at[len(copies)]))
    for copy in copies:
        copy.start()
    for copy in copies:
        copy.wait()


def fused(adj_e, adj_h, fwd_e, permittivity, design_mask, inverse, omega, port_mode, port_plane):
    n = lax.axis_size("line")
    cells, strip = (inverse.shape[0], adj_e.shape[2])
    steps = fwd_e.shape[0]
    hbm = pl.BlockSpec(memory_space=pltpu.HBM)
    vmem = pl.BlockSpec(memory_space=pltpu.VMEM)
    smem = pl.BlockSpec(memory_space=pltpu.SMEM)
    scratch = [
        pltpu.VMEM((3, strip, cells), F32),
        pltpu.VMEM((3, strip, cells), F32),
        pltpu.VMEM((steps, 3, strip, cells), BF16),
        pltpu.VMEM((strip, cells), F32),
        pltpu.VMEM((strip, cells), jnp.int32),
        pltpu.VMEM((cells, cells), BF16),
        pltpu.VMEM((8, cells), F32),
        pltpu.VMEM((8, cells), F32),
        pltpu.VMEM((8, cells), F32),
        pltpu.VMEM((n, strip // 2, LANES), F32),
        pltpu.VMEM((n, strip // 2, LANES), F32),
        pltpu.VMEM((cells, LANES), F32),
        pltpu.VMEM((cells + PAD, LANES), F32),
        pltpu.VMEM((cells + PAD, LANES), F32),
        pltpu.VMEM((strip, cells), F32),
        pltpu.VMEM((cells // LANES, LANES), F32),
        pltpu.VMEM((cells + PAD, LANES), F32),
        pltpu.VMEM((6 * strip, cells), BF16),
        pltpu.VMEM((3, cells + 2 * PAD, LANES), F32),
        pltpu.VMEM((cells, LANES), F32),
        pltpu.VMEM((9, n, strip, LANES), BF16),
        pltpu.VMEM((9, n, strip, LANES), BF16),
        pltpu.VMEM((strip, cells), F32),
        pltpu.SemaphoreType.DMA((7,)),
        pltpu.SemaphoreType.DMA((2,)),
        pltpu.SemaphoreType.DMA((2,)),
        pltpu.SemaphoreType.DMA((n,)),
        pltpu.SemaphoreType.DMA((n,)),
        pltpu.SemaphoreType.DMA((9, n)),
        pltpu.SemaphoreType.DMA((9, n)),
    ]
    shapes = tuple(jax.ShapeDtypeStruct(a.shape, F32) for a in (adj_e, adj_h, permittivity))
    results = pl.pallas_call(
        functools.partial(kernel, n),
        out_shape=tuple(pltpu.VMEM(a.shape, F32) for a in shapes),
        in_specs=[hbm] * 6 + [smem, hbm, smem],
        out_specs=(vmem, vmem, vmem),
        scratch_shapes=scratch,
        compiler_params=pltpu.CompilerParams(
            collective_id=0, has_side_effects=True, vmem_limit_bytes=60 * 1024 * 1024
        ),
    )(
        adj_e, adj_h, fwd_e, permittivity, design_mask, inverse, omega,
        port_mode.reshape(cells // LANES, LANES), port_plane,
    )
    return tuple(
        pl.pallas_call(
            write_out,
            out_shape=shapes,
            in_specs=[pl.BlockSpec(memory_space=pl.ANY)] * 3,
            out_specs=(hbm, hbm, hbm),
            scratch_shapes=[pltpu.SemaphoreType.DMA((7,))],
        )(*results)
    )


def per_device(adj_e, adj_h, fwd_e, permittivity, design_mask, inverse, omega, port_mode, port_plane):
    args = (adj_e, adj_h, fwd_e, permittivity, design_mask, inverse, omega, port_mode, port_plane)
    paired = 2 * adj_e.shape[2] == LANES and fwd_e.shape[0] == 2 and permittivity.shape[0] == 1
    return fused(*args) if paired else plain_per_device(*args)


def solution(mesh):
    in_specs = (
        P(None, "exc", "line", None),
        P(None, "exc", "line", None),
        P(None, None, "exc", "line", None),
        P(None, "line", None),
        P(None, "line", None),
        P(),
        P("exc"),
        P("exc"),
        P("exc"),
    )
    out_specs = (P(None, "exc", "line", None), P(None, "exc", "line", None), P("exc", "line", None))
    return jax.shard_map(
        per_device, mesh=mesh, in_specs=in_specs, out_specs=out_specs, check_vma=False
    )
```

```python
import functools

import jax
import jax.numpy as jnp
from jax import lax
from jax.experimental import pallas as pl
from jax.experimental.pallas import tpu as pltpu
from jax.sharding import PartitionSpec as P

COURANT = 0.4


def extended(array, sides, width):
    for axis, dim in sides:
        devices, length = (lax.axis_size(axis), array.shape[dim])
        up = [(i, (i + 1) % devices) for i in range(devices - 1)]
        down = [(j, i) for i, j in up]
        last = lax.slice_in_dim(array, length - width, length, axis=dim)
        first = lax.slice_in_dim(array, 0, width, axis=dim)
        before = lax.ppermute(last, axis, up)
        after = lax.ppermute(first, axis, down)
        array = jnp.concatenate([before, array, after], axis=dim)
    return array


def lower_diff(padded, along):
    inner = padded.shape[along] - 2
    middle = lax.slice_in_dim(padded, 1, inner + 1, axis=along)
    return middle - lax.slice_in_dim(padded, 0, inner, axis=along)


def upper_diff(padded, along):
    inner = padded.shape[along] - 2
    middle = lax.slice_in_dim(padded, 1, inner + 1, axis=along)
    return lax.slice_in_dim(padded, 2, inner + 2, axis=along) - middle


def zero_rim(stacked, along):
    widths = [(0, 0)] * stacked.ndim
    widths[along] = (1, 1)
    return jnp.pad(stacked, widths)


def row_rim(stacked, along):
    return extended(stacked, (("line", 2),), 1)


def column_rim(stacked, along):
    return extended(stacked, (("line", 2),), 1)


def curl_along_y(fields, inverse_eps, extend, along):
    electric_x, electric_y, electric_z = (fields[0], fields[1], fields[2])
    magnetic_x, magnetic_y, magnetic_z = (fields[3], fields[4], fields[5])
    scaled = COURANT * inverse_eps
    lower_terms = lower_diff(extend(jnp.stack([magnetic_x, magnetic_z]), along), along)
    electric_x = electric_x + scaled * lower_terms[1]
    electric_z = electric_z - scaled * lower_terms[0]
    upper_terms = upper_diff(extend(jnp.stack([electric_x, electric_z]), along), along)
    magnetic_x = magnetic_x - COURANT * upper_terms[1]
    magnetic_z = magnetic_z + COURANT * upper_terms[0]
    return jnp.stack([electric_x, electric_y, electric_z, magnetic_x, magnetic_y, magnetic_z])


def curl_along_xz(fields, inverse_eps, extend, along):
    electric_x, electric_y, electric_z = (fields[0], fields[1], fields[2])
    magnetic_x, magnetic_y, magnetic_z = (fields[3], fields[4], fields[5])
    scaled = COURANT * inverse_eps
    depth_terms = lower_diff(zero_rim(jnp.stack([magnetic_x, magnetic_y]), 1), 1)
    across = lower_diff(extend(jnp.stack([magnetic_y, magnetic_z]), along), along)
    electric_x = electric_x - scaled * depth_terms[1]
    electric_y = electric_y + scaled * (depth_terms[0] - across[1])
    electric_z = electric_z + scaled * across[0]
    depth_upper = upper_diff(zero_rim(jnp.stack([electric_x, electric_y]), 1), 1)
    across_upper = upper_diff(extend(jnp.stack([electric_y, electric_z]), along), along)
    magnetic_x = magnetic_x + COURANT * depth_upper[1]
    magnetic_y = magnetic_y + COURANT * (across_upper[1] - depth_upper[0])
    magnetic_z = magnetic_z - COURANT * across_upper[0]
    return jnp.stack([electric_x, electric_y, electric_z, magnetic_x, magnetic_y, magnetic_z])


def line_solve(rounded, inverse):
    flattened = rounded.reshape(-1, rounded.shape[-1])
    solved = lax.dot_general(
        flattened, inverse, (((1,), (1,)), ((), ())), preferred_element_type=jnp.float32
    )
    return solved.reshape(rounded.shape)


def fold_lines(field, line_count):
    strip_width = field.shape[-2]
    block = field.shape[-1] // line_count
    regrouped = field.reshape(field.shape[:-2] + (strip_width, line_count, block))
    regrouped = jnp.moveaxis(regrouped, -3, -1)
    return regrouped.reshape(field.shape[:-2] + (line_count, block * strip_width))


def unfold(received, block):
    line_count = received.shape[-2]
    strip_width = received.shape[-1] // block
    regrouped = received.reshape(received.shape[:-2] + (line_count, block, strip_width))
    regrouped = jnp.moveaxis(regrouped, -3, -2)
    return regrouped.reshape(received.shape[:-2] + (block, line_count * strip_width))


def accumulate(gradient, fields, snapshot, mask_weight, inverse_cols):
    forward = snapshot.astype(jnp.float32)
    intersection = fields[0] * forward[0] + fields[1] * forward[1] + fields[2] * forward[2]
    return gradient + mask_weight * intersection * (inverse_cols * inverse_cols)


def plain_per_device(
    adj_e, adj_h, fwd_e, permittivity, design_mask, inverse, omega, port_mode, port_plane
):
    line_cells = inverse.shape[0]
    strip_width = adj_e.shape[2]
    step_count = fwd_e.shape[0]
    line_count = lax.axis_size("line")
    fields = jnp.concatenate([adj_e, adj_h], 0)
    inverse_rows = 1.0 / permittivity
    eps_turned = lax.all_to_all(
        fold_lines(permittivity, line_count), "line", split_axis=1, concat_axis=1, tiled=True
    )
    inverse_cols = 1.0 / unfold(eps_turned, strip_width)
    frequency = omega[0]
    plane_at = port_plane[0]
    offset = lax.axis_index("line") * strip_width
    column = (jnp.arange(line_cells, dtype=jnp.int32) == plane_at).astype(jnp.float32)
    profile_rows = lax.dynamic_slice_in_dim(port_mode, offset, strip_width)
    mask_weight = design_mask.astype(jnp.float32)
    gradient = jnp.zeros(permittivity.shape, jnp.float32)
    for instant in range(step_count):
        amplitude = jnp.cos(frequency * (instant + 1))
        fields = fields.at[2].add(amplitude * profile_rows[None, :, None] * column[None, None, :])
        fields = curl_along_y(fields, inverse_rows, row_rim, 2)
        fields = line_solve(fields.astype(jnp.bfloat16), inverse)
        turned = unfold(
            lax.all_to_all(
                fold_lines(fields, line_count), "line", split_axis=2, concat_axis=2, tiled=True
            ),
            strip_width,
        )
        turned = curl_along_xz(turned, inverse_cols, column_rim, 2)
        turned = line_solve(turned.astype(jnp.bfloat16), inverse)
        gradient = accumulate(gradient, turned, fwd_e[instant], mask_weight, inverse_cols)
        if instant + 1 < step_count:
            fields = unfold(
                lax.all_to_all(
                    fold_lines(turned, line_count), "line", split_axis=2, concat_axis=2, tiled=True
                ),
                strip_width,
            )
    return (turned[:3], turned[3:], gradient)


LANES = 128
MESH = pl.DeviceIdType.MESH
PAD = 8
F32, BF16 = (jnp.float32, jnp.bfloat16)


def contract(left, right):
    return lax.dot_general(left, right, (((1,), (1,)), ((), ())), preferred_element_type=F32)


def shifted_down(value, first):
    row = lax.broadcasted_iota(jnp.int32, value.shape, 0)
    return jnp.where(row == 0, first, pltpu.roll(value, 1, 0))


def shifted_up(value, last):
    rows = value.shape[0]
    row = lax.broadcasted_iota(jnp.int32, value.shape, 0)
    return jnp.where(row == rows - 1, last, pltpu.roll(value, rows - 1, 0))


def kernel(
    n, e_hbm, h_hbm, fwd_hbm, perm_hbm, mask_hbm, inv_hbm, omega, mode_hbm, plane,
    oe, oh, og,
    e, h, fwd, perm, mask, inv, halo, halo_lo, halo_hi, p_send, p_recv, eps_t, r_first, r_second, inv_eps,
    mode_v, mode_col, lines, solved, kept, send, recv, send_two, recv_two, grad,
    load_sem, halo_send_sem, halo_recv_sem, p_send_sem, p_recv_sem, send_sem, recv_sem,
):
    me = lax.axis_index("line")
    strip = perm.shape[0]
    cells = inv.shape[0]
    above, below = (lax.rem(me + 1, n), lax.rem(me + n - 1, n))

    barrier = pltpu.get_barrier_semaphore()

    far = sorted(range(1, n), key=lambda k: -min(k, n - k))
    turns = [k for two in zip(far, far[::-1]) for k in two][: n - 1]
    others = [lax.rem(me + k, n) for k in turns]
    for other in others:
        pl.semaphore_signal(barrier, inc=1, device_id={"line": other}, device_id_type=MESH)

    loads = []
    for source, target in (
        (perm_hbm.at[0], perm), (mode_hbm, mode_v), (e_hbm.at[:, 0], e), (h_hbm.at[:, 0], h), (inv_hbm, inv),
        (fwd_hbm.at[:, :, 0], fwd), (mask_hbm.at[0], mask),
    ):
        copy = pltpu.make_async_copy(source, target, load_sem.at[len(loads)])
        copy.start()
        loads.append(copy)

    lane = lax.broadcasted_iota(jnp.int32, (1, LANES), 1)
    low = lane < strip

    loads[0].wait()
    twice = jnp.concatenate([perm[...], perm[...]], 0)
    eps_t[...] = twice.T
    for block in range(n):
        first = eps_t[block * strip : block * strip + strip // 2, :]
        second = eps_t[block * strip + strip // 2 : (block + 1) * strip, :]
        p_send[block] = jnp.where(low, first, second)
    r_first[0:cells, :] = COURANT * (1.0 / eps_t[...])
    r_first[cells:, :] = jnp.zeros((PAD, LANES), F32)

    loads[1].wait()
    for block in range(cells // LANES):
        line = jnp.broadcast_to(mode_v[block : block + 1, :], (LANES, LANES))
        mode_col[block * LANES : (block + 1) * LANES, :] = line.T
    mode_col[cells:, :] = jnp.zeros((PAD, LANES), F32)
    amplitudes = [jnp.cos(jnp.full((1, LANES), omega[0] * (s + 1), F32)) for s in range(2)]
    at_plane = plane[0]

    loads[2].wait()
    loads[3].wait()
    halo[...] = jnp.concatenate(
        [
            e[0, 0:1, :], e[2, 0:1, :], h[0, 0:1, :], h[2, 0:1, :], perm[0:1, :],
            h[0, strip - 1 : strip, :], h[2, strip - 1 : strip, :], perm[0:1, :],
        ],
        0,
    )

    pl.semaphore_wait(barrier, n - 1)

    to_above = pltpu.make_async_remote_copy(
        halo, halo_lo, halo_send_sem.at[0], halo_recv_sem.at[0], device_id={"line": above}, device_id_type=MESH
    )
    to_below = pltpu.make_async_remote_copy(
        halo, halo_hi, halo_send_sem.at[1], halo_recv_sem.at[1], device_id={"line": below}, device_id_type=MESH
    )
    to_above.start()
    to_below.start()

    def p_copy(to, slot):
        return pltpu.make_async_remote_copy(
            p_send.at[to], p_recv.at[slot], p_send_sem.at[to], p_recv_sem.at[slot],
            device_id={"line": to}, device_id_type=MESH,
        )

    for other in others:
        p_copy(other, me).start()
    p_recv[me] = p_send[me]

    to_above.wait()
    to_below.wait()
    is_first, is_last = (me == 0, me == n - 1)
    x_at = lax.broadcasted_iota(jnp.int32, (1, cells), 1)
    column = jnp.where(x_at == at_plane, 1.0, 0.0)
    profile = mode_col[pl.ds(pl.multiple_of(me * strip, strip), strip + PAD), :] * amplitudes[0]
    profile = jnp.concatenate([profile] * (cells // LANES), 1)
    source = profile * column
    r = COURANT * (1.0 / perm[...])
    ex, ez, hx, hz = (e[0], e[2] + source[0:strip], h[0], h[2])
    hx_lo = jnp.where(is_first, 0.0, halo_lo[5:6, :])
    hz_lo = jnp.where(is_first, 0.0, halo_lo[6:7, :])
    ex = ex + r * (hz - shifted_down(hz, hz_lo))
    ez = ez - r * (hx - shifted_down(hx, hx_lo))
    r_hi = COURANT * (1.0 / halo_hi[4:5, :])
    ex_hi = halo_hi[0:1, :] + r_hi * (halo_hi[3:4, :] - hz[strip - 1 : strip])
    ez_hi = halo_hi[1:2, :] + source[strip : strip + 1] - r_hi * (halo_hi[2:3, :] - hx[strip - 1 : strip])
    ex_hi = jnp.where(is_last, 0.0, ex_hi)
    ez_hi = jnp.where(is_last, 0.0, ez_hi)
    hx = hx - COURANT * (shifted_up(ez, ez_hi) - ez)
    hz = hz + COURANT * (shifted_up(ex, ex_hi) - ex)
    for at, value in enumerate((ex, ez, h[1], e[1], hz, hx)):
        lines[at * strip : (at + 1) * strip, :] = value.astype(BF16)

    groups = ((0, 2), (2, 1), (3, 1), (4, 1), (5, 1), (6, 1), (7, 2))

    def copy_out(group, to, slot):
        first, count = groups[group]
        if count == 2:
            out, into = (send_two.at[first // 7, to], recv_two.at[first // 7, slot])
        else:
            out, into = (send.at[first - 2, to], recv.at[first - 2, slot])
        return pltpu.make_async_remote_copy(
            out, into, send_sem.at[group, to], recv_sem.at[group, slot],
            device_id={"line": to}, device_id_type=MESH,
        )

    def tile_at(tile, one, two, device):
        if 2 <= tile <= 6:
            return one.at[tile - 2, device]
        return two.at[tile // 7, device, (tile - 7 if tile >= 7 else tile)]

    def send_all(group):
        for other in others:
            copy_out(group, other, me).start()
        first, count = groups[group]
        for tile in range(first, first + count):
            tile_at(tile, recv, recv_two, me)[...] = tile_at(tile, send, send_two, me)[...]

    def receive_all(group):
        def take(k, carry):
            other = lax.rem(me + k, n)
            copy_out(group, other, other).wait_recv()
            return carry

        lax.fori_loop(1, n, take, 0)

    def assemble(message, tile):
        at = tile * LANES
        for k in range(n // 2):
            a, b = [tile_at(message, recv, recv_two, 2 * k + odd)[...] for odd in range(2)]
            cut = slice(k * LANES, (k + 1) * LANES)
            lines[at : at + strip, cut] = jnp.concatenate([a[:, :strip], b[:, :strip]], 1)
            lines[at + strip : at + LANES, cut] = jnp.concatenate([a[:, strip:], b[:, strip:]], 1)

    def solve_tile(tile):
        part = lines[tile * LANES : (tile + 1) * LANES, :]
        solved[tile, PAD : cells + PAD, :] = contract(inv[...], part)

    rows = LANES

    def put(message, start, tile):
        for part in range(rows // strip):
            target = tile_at(message, send, send_two, start // strip + part)
            target[...] = tile[part * strip : (part + 1) * strip].astype(BF16)

    def swap(tile):
        return pltpu.roll(tile, LANES // 2, 1)

    def extended(tile, start, back):
        return solved[tile, start + PAD - back : start + PAD - back + rows + PAD, :]

    def next_row(value):
        return pltpu.roll(value, value.shape[0] - 1, 0)

    def in_grid(start):
        return lax.broadcasted_iota(jnp.int32, (rows + PAD, LANES), 0) + start < cells

    def curl_x_first(start):
        here = slice(start + PAD, start + PAD + rows)
        b, bd = (solved[1, here, :], solved[1, start + PAD - 1 : start + PAD - 1 + rows, :])
        hy, hyd = (jnp.where(low, b, swap(b)), jnp.where(low, bd, swap(bd)))
        a = solved[0, here, :] + r_first[start : start + rows, :] * jnp.where(low, -hy, hy - hyd)
        solved[0, here, :] = a
        return a

    def curl_x_second(start):
        a, b, c = (extended(0, start, 0), extended(1, start, 0), extended(2, start, 0))
        sa, sc = (swap(a), swap(c))
        dc = sc - swap(extended(2, start, 1))
        ey = b + r_first[start : start + rows + PAD, :] * (c - dc)
        ey = jnp.where(in_grid(start), ey, 0.0)
        hy = b + COURANT * ((next_row(sa) - sa) + a)
        sy = swap(ey)
        c = c - COURANT * jnp.where(low, next_row(sy) - sy, ey)
        return jnp.where(low, hy, ey)[0:rows], c[0:rows]

    def curl_y(tile, start, sign, source):
        t, td = (extended(tile, start, 0), extended(tile, start, 1))
        st, std = (swap(t), swap(td))
        p = t if source is None else t + source
        p = p + sign * r_second[start : start + rows + PAD, :] * (st - std)
        p = jnp.where(in_grid(start), p, 0.0)
        sp = swap(p)
        q = t + sign * COURANT * (next_row(sp) - sp)
        return jnp.where(low, p, q)[0:rows]

    def along(electric, instant):
        return (
            electric[0] * fwd[instant, 0].astype(F32)
            + electric[1] * fwd[instant, 1].astype(F32)
            + electric[2] * fwd[instant, 2].astype(F32)
        )

    for tile in range(3):
        solved[tile, 0:PAD, :] = jnp.zeros((PAD, LANES), F32)
        solved[tile, cells + PAD :, :] = jnp.zeros((PAD, LANES), F32)
    starts = range(0, cells, rows)

    loads[4].wait()
    result = contract(inv[...], lines[...])
    for tile in range(3):
        solved[tile, PAD : cells + PAD, :] = result[:, tile * LANES : (tile + 1) * LANES]
    for start in starts:
        curl_x_first(start)
    for start in starts:
        a = solved[0, start + PAD : start + PAD + rows, :]
        b, c = curl_x_second(start)
        put(0, start, jnp.where(low, a, swap(c)))
        put(1, start, jnp.where(low, swap(a), c))
        put(2, start, b)
    send_all(0)
    send_all(1)

    def p_take(k, carry):
        other = lax.rem(me + k, n)
        p_copy(other, other).wait_recv()
        return carry

    lax.fori_loop(1, n, p_take, 0)
    for k in range(n // 2):
        a, b = (p_recv[2 * k], p_recv[2 * k + 1])
        cut = slice(k * LANES, (k + 1) * LANES)
        inv_eps[0 : strip // 2, cut] = 1.0 / jnp.concatenate([a[:, :strip], b[:, :strip]], 1)
        inv_eps[strip // 2 :, cut] = 1.0 / jnp.concatenate([a[:, strip:], b[:, strip:]], 1)
    both = jnp.concatenate([inv_eps[...], inv_eps[...]], 0)
    r_second[0:cells, :] = COURANT * both.T
    r_second[cells:, :] = jnp.zeros((PAD, LANES), F32)
    loads[5].wait()
    loads[6].wait()

    receive_all(0)
    assemble(0, 0)
    solve_tile(0)
    for start in starts:
        kept[start : start + rows, :] = curl_y(0, start, 1.0, None)
    assemble(1, 1)
    solve_tile(1)
    here = jnp.where(low & (lane + me * strip == at_plane), 1.0, 0.0)
    for start in starts:
        source = (amplitudes[1] * mode_col[start : start + rows + PAD, :]) * here
        b = curl_y(1, start, -1.0, source)
        a = kept[start : start + rows, :]
        put(3, start, jnp.where(low, a, swap(b)))
        put(5, start, jnp.where(low, swap(a), b))
    send_all(2)
    receive_all(1)
    assemble(2, 2)
    solve_tile(2)
    for start in starts:
        put(4, start, solved[2, start + PAD : start + PAD + rows, :])
    send_all(3)
    send_all(4)

    weight = mask[...].astype(F32)
    square = inv_eps[...] * inv_eps[...]
    electric = jnp.concatenate(
        [lines[0:strip, :], lines[LANES + strip * 0 : LANES + strip, :], lines[2 * LANES + strip :, :]], 0
    )
    electric = contract(electric, inv[...])
    parts = (electric[0:strip], electric[2 * strip :], electric[strip : 2 * strip])
    grad[...] = weight * along(parts, 0) * square

    for tile in range(2):
        receive_all(2 + tile)
        assemble(3 + tile, tile)
        solve_tile(tile)
    for start in starts:
        put(6, start, curl_x_first(start))
    send_all(5)
    receive_all(4)
    assemble(5, 2)
    solve_tile(2)
    for start in starts:
        b, c = curl_x_second(start)
        put(7, start, b)
        put(8, start, c)
    send_all(6)

    receive_all(5)
    assemble(6, 0)
    pair = contract(lines[0:LANES, :], inv[...])
    oe[0, 0] = pair[:strip]
    oe[2, 0] = pair[strip:]
    receive_all(6)
    assemble(7, 1)
    pair = contract(lines[LANES : 2 * LANES, :], inv[...])
    oh[1, 0] = pair[:strip]
    oe[1, 0] = pair[strip:]
    og[0] = grad[...] + weight * along((oe[0, 0], pair[strip:], oe[2, 0]), 1) * square
    assemble(8, 2)
    pair = contract(lines[2 * LANES :, :], inv[...])
    oh[2, 0] = pair[:strip]
    oh[0, 0] = pair[strip:]

    def settle(k, carry):
        other = lax.rem(me + k, n)
        p_copy(other, other).wait_send()
        for group in range(len(groups)):
            copy_out(group, other, other).wait_send()
        return carry

    lax.fori_loop(1, n, settle, 0)


def write_out(e, h, g, oe, oh, og, sem):
    copies = []
    for source, target in ((e, oe), (h, oh)):
        for at in range(3):
            copies.append(pltpu.make_async_copy(source.at[at], target.at[at], sem.at[len(copies)]))
    copies.append(pltpu.make_async_copy(g, og, sem.at[len(copies)]))
    for copy in copies:
        copy.start()
    for copy in copies:
        copy.wait()


def fused(adj_e, adj_h, fwd_e, permittivity, design_mask, inverse, omega, port_mode, port_plane):
    n = lax.axis_size("line")
    cells, strip = (inverse.shape[0], adj_e.shape[2])
    steps = fwd_e.shape[0]
    hbm = pl.BlockSpec(memory_space=pltpu.HBM)
    vmem = pl.BlockSpec(memory_space=pltpu.VMEM)
    smem = pl.BlockSpec(memory_space=pltpu.SMEM)
    scratch = [
        pltpu.VMEM((3, strip, cells), F32),
        pltpu.VMEM((3, strip, cells), F32),
        pltpu.VMEM((steps, 3, strip, cells), BF16),
        pltpu.VMEM((strip, cells), F32),
        pltpu.VMEM((strip, cells), jnp.int32),
        pltpu.VMEM((cells, cells), BF16),
        pltpu.VMEM((8, cells), F32),
        pltpu.VMEM((8, cells), F32),
        pltpu.VMEM((8, cells), F32),
        pltpu.VMEM((n, strip // 2, LANES), F32),
        pltpu.VMEM((n, strip // 2, LANES), F32),
        pltpu.VMEM((cells, LANES), F32),
        pltpu.VMEM((cells + PAD, LANES), F32),
        pltpu.VMEM((cells + PAD, LANES), F32),
        pltpu.VMEM((strip, cells), F32),
        pltpu.VMEM((cells // LANES, LANES), F32),
        pltpu.VMEM((cells + PAD, LANES), F32),
        pltpu.VMEM((6 * strip, cells), BF16),
        pltpu.VMEM((3, cells + 2 * PAD, LANES), F32),
        pltpu.VMEM((cells, LANES), F32),
        pltpu.VMEM((5, n, strip, LANES), BF16),
        pltpu.VMEM((5, n, strip, LANES), BF16),
        pltpu.VMEM((2, n, 2, strip, LANES), BF16),
        pltpu.VMEM((2, n, 2, strip, LANES), BF16),
        pltpu.VMEM((strip, cells), F32),
        pltpu.SemaphoreType.DMA((7,)),
        pltpu.SemaphoreType.DMA((2,)),
        pltpu.SemaphoreType.DMA((2,)),
        pltpu.SemaphoreType.DMA((n,)),
        pltpu.SemaphoreType.DMA((n,)),
        pltpu.SemaphoreType.DMA((7, n)),
        pltpu.SemaphoreType.DMA((7, n)),
    ]
    shapes = tuple(jax.ShapeDtypeStruct(a.shape, F32) for a in (adj_e, adj_h, permittivity))
    results = pl.pallas_call(
        functools.partial(kernel, n),
        out_shape=tuple(pltpu.VMEM(a.shape, F32) for a in shapes),
        in_specs=[hbm] * 6 + [smem, hbm, smem],
        out_specs=(vmem, vmem, vmem),
        scratch_shapes=scratch,
        compiler_params=pltpu.CompilerParams(
            collective_id=0, has_side_effects=True, vmem_limit_bytes=60 * 1024 * 1024
        ),
    )(
        adj_e, adj_h, fwd_e, permittivity, design_mask, inverse, omega,
        port_mode.reshape(cells // LANES, LANES), port_plane,
    )
    return tuple(
        pl.pallas_call(
            write_out,
            out_shape=shapes,
            in_specs=[pl.BlockSpec(memory_space=pl.ANY)] * 3,
            out_specs=(hbm, hbm, hbm),
            scratch_shapes=[pltpu.SemaphoreType.DMA((7,))],
            compiler_params=pltpu.CompilerParams(vmem_limit_bytes=1024 * 1024),
        )(*results)
    )


def per_device(adj_e, adj_h, fwd_e, permittivity, design_mask, inverse, omega, port_mode, port_plane):
    args = (adj_e, adj_h, fwd_e, permittivity, design_mask, inverse, omega, port_mode, port_plane)
    paired = 2 * adj_e.shape[2] == LANES and fwd_e.shape[0] == 2 and permittivity.shape[0] == 1
    return fused(*args) if paired else plain_per_device(*args)


def solution(mesh):
    in_specs = (
        P(None, "exc", "line", None),
        P(None, "exc", "line", None),
        P(None, None, "exc", "line", None),
        P(None, "line", None),
        P(None, "line", None),
        P(),
        P("exc"),
        P("exc"),
        P("exc"),
    )
    out_specs = (P(None, "exc", "line", None), P(None, "exc", "line", None), P("exc", "line", None))
    return jax.shard_map(
        per_device, mesh=mesh, in_specs=in_specs, out_specs=out_specs, check_vma=False
    )
```

```python
import functools

import jax
import jax.numpy as jnp
from jax import lax
from jax.experimental import pallas as pl
from jax.experimental.pallas import tpu as pltpu
from jax.sharding import PartitionSpec as P

COURANT = 0.4


def extended(array, sides, width):
    for axis, dim in sides:
        devices, length = (lax.axis_size(axis), array.shape[dim])
        up = [(i, (i + 1) % devices) for i in range(devices - 1)]
        down = [(j, i) for i, j in up]
        last = lax.slice_in_dim(array, length - width, length, axis=dim)
        first = lax.slice_in_dim(array, 0, width, axis=dim)
        before = lax.ppermute(last, axis, up)
        after = lax.ppermute(first, axis, down)
        array = jnp.concatenate([before, array, after], axis=dim)
    return array


def lower_diff(padded, along):
    inner = padded.shape[along] - 2
    middle = lax.slice_in_dim(padded, 1, inner + 1, axis=along)
    return middle - lax.slice_in_dim(padded, 0, inner, axis=along)


def upper_diff(padded, along):
    inner = padded.shape[along] - 2
    middle = lax.slice_in_dim(padded, 1, inner + 1, axis=along)
    return lax.slice_in_dim(padded, 2, inner + 2, axis=along) - middle


def zero_rim(stacked, along):
    widths = [(0, 0)] * stacked.ndim
    widths[along] = (1, 1)
    return jnp.pad(stacked, widths)


def row_rim(stacked, along):
    return extended(stacked, (("line", 2),), 1)


def column_rim(stacked, along):
    return extended(stacked, (("line", 2),), 1)


def curl_along_y(fields, inverse_eps, extend, along):
    electric_x, electric_y, electric_z = (fields[0], fields[1], fields[2])
    magnetic_x, magnetic_y, magnetic_z = (fields[3], fields[4], fields[5])
    scaled = COURANT * inverse_eps
    lower_terms = lower_diff(extend(jnp.stack([magnetic_x, magnetic_z]), along), along)
    electric_x = electric_x + scaled * lower_terms[1]
    electric_z = electric_z - scaled * lower_terms[0]
    upper_terms = upper_diff(extend(jnp.stack([electric_x, electric_z]), along), along)
    magnetic_x = magnetic_x - COURANT * upper_terms[1]
    magnetic_z = magnetic_z + COURANT * upper_terms[0]
    return jnp.stack([electric_x, electric_y, electric_z, magnetic_x, magnetic_y, magnetic_z])


def curl_along_xz(fields, inverse_eps, extend, along):
    electric_x, electric_y, electric_z = (fields[0], fields[1], fields[2])
    magnetic_x, magnetic_y, magnetic_z = (fields[3], fields[4], fields[5])
    scaled = COURANT * inverse_eps
    depth_terms = lower_diff(zero_rim(jnp.stack([magnetic_x, magnetic_y]), 1), 1)
    across = lower_diff(extend(jnp.stack([magnetic_y, magnetic_z]), along), along)
    electric_x = electric_x - scaled * depth_terms[1]
    electric_y = electric_y + scaled * (depth_terms[0] - across[1])
    electric_z = electric_z + scaled * across[0]
    depth_upper = upper_diff(zero_rim(jnp.stack([electric_x, electric_y]), 1), 1)
    across_upper = upper_diff(extend(jnp.stack([electric_y, electric_z]), along), along)
    magnetic_x = magnetic_x + COURANT * depth_upper[1]
    magnetic_y = magnetic_y + COURANT * (across_upper[1] - depth_upper[0])
    magnetic_z = magnetic_z - COURANT * across_upper[0]
    return jnp.stack([electric_x, electric_y, electric_z, magnetic_x, magnetic_y, magnetic_z])


def line_solve(rounded, inverse):
    flattened = rounded.reshape(-1, rounded.shape[-1])
    solved = lax.dot_general(
        flattened, inverse, (((1,), (1,)), ((), ())), preferred_element_type=jnp.float32
    )
    return solved.reshape(rounded.shape)


def fold_lines(field, line_count):
    strip_width = field.shape[-2]
    block = field.shape[-1] // line_count
    regrouped = field.reshape(field.shape[:-2] + (strip_width, line_count, block))
    regrouped = jnp.moveaxis(regrouped, -3, -1)
    return regrouped.reshape(field.shape[:-2] + (line_count, block * strip_width))


def unfold(received, block):
    line_count = received.shape[-2]
    strip_width = received.shape[-1] // block
    regrouped = received.reshape(received.shape[:-2] + (line_count, block, strip_width))
    regrouped = jnp.moveaxis(regrouped, -3, -2)
    return regrouped.reshape(received.shape[:-2] + (block, line_count * strip_width))


def accumulate(gradient, fields, snapshot, mask_weight, inverse_cols):
    forward = snapshot.astype(jnp.float32)
    intersection = fields[0] * forward[0] + fields[1] * forward[1] + fields[2] * forward[2]
    return gradient + mask_weight * intersection * (inverse_cols * inverse_cols)


def plain_per_device(
    adj_e, adj_h, fwd_e, permittivity, design_mask, inverse, omega, port_mode, port_plane
):
    line_cells = inverse.shape[0]
    strip_width = adj_e.shape[2]
    step_count = fwd_e.shape[0]
    line_count = lax.axis_size("line")
    fields = jnp.concatenate([adj_e, adj_h], 0)
    inverse_rows = 1.0 / permittivity
    eps_turned = lax.all_to_all(
        fold_lines(permittivity, line_count), "line", split_axis=1, concat_axis=1, tiled=True
    )
    inverse_cols = 1.0 / unfold(eps_turned, strip_width)
    frequency = omega[0]
    plane_at = port_plane[0]
    offset = lax.axis_index("line") * strip_width
    column = (jnp.arange(line_cells, dtype=jnp.int32) == plane_at).astype(jnp.float32)
    profile_rows = lax.dynamic_slice_in_dim(port_mode, offset, strip_width)
    mask_weight = design_mask.astype(jnp.float32)
    gradient = jnp.zeros(permittivity.shape, jnp.float32)
    for instant in range(step_count):
        amplitude = jnp.cos(frequency * (instant + 1))
        fields = fields.at[2].add(amplitude * profile_rows[None, :, None] * column[None, None, :])
        fields = curl_along_y(fields, inverse_rows, row_rim, 2)
        fields = line_solve(fields.astype(jnp.bfloat16), inverse)
        turned = unfold(
            lax.all_to_all(
                fold_lines(fields, line_count), "line", split_axis=2, concat_axis=2, tiled=True
            ),
            strip_width,
        )
        turned = curl_along_xz(turned, inverse_cols, column_rim, 2)
        turned = line_solve(turned.astype(jnp.bfloat16), inverse)
        gradient = accumulate(gradient, turned, fwd_e[instant], mask_weight, inverse_cols)
        if instant + 1 < step_count:
            fields = unfold(
                lax.all_to_all(
                    fold_lines(turned, line_count), "line", split_axis=2, concat_axis=2, tiled=True
                ),
                strip_width,
            )
    return (turned[:3], turned[3:], gradient)


LANES = 128
MESH = pl.DeviceIdType.MESH
PAD = 8
EDGE = 16
F32, BF16 = (jnp.float32, jnp.bfloat16)


def contract(left, right):
    return lax.dot_general(left, right, (((1,), (1,)), ((), ())), preferred_element_type=F32)


def shifted_down(value, first):
    row = lax.broadcasted_iota(jnp.int32, value.shape, 0)
    return jnp.where(row == 0, first, pltpu.roll(value, 1, 0))


def shifted_up(value, last):
    rows = value.shape[0]
    row = lax.broadcasted_iota(jnp.int32, value.shape, 0)
    return jnp.where(row == rows - 1, last, pltpu.roll(value, rows - 1, 0))


def kernel(
    n, e_hbm, h_hbm, fwd_hbm, perm_hbm, mask_hbm, inv_hbm, omega, mode_hbm, plane,
    oe, oh, og,
    e, h, fwd, perm, mask, inv, halo, halo_lo, halo_hi, p_send, p_recv, eps_t, r_first, r_second, inv_eps,
    mode_v, mode_col, lines, solved, kept, send, recv, send_two, recv_two, grad,
    load_sem, hand_sem, halo_send_sem, halo_recv_sem, p_send_sem, p_recv_sem, send_sem, recv_sem,
):
    me, core = (lax.axis_index("line"), lax.axis_index("exc"))
    strip = perm.shape[0]
    cells = perm.shape[1]
    half = strip // 4
    inverse = inv.at[EDGE : cells + EDGE]
    above, below = (lax.rem(me + 1, n), lax.rem(me + n - 1, n))

    barrier = pltpu.get_barrier_semaphore()

    far = sorted(range(1, n), key=lambda k: -min(k, n - k))
    turns = [k for two in zip(far, far[::-1]) for k in two][: n - 1]
    others = [lax.rem(me + k, n) for k in turns]
    for other in others:
        pl.semaphore_signal(barrier, inc=1, device_id={"line": other}, device_id_type=MESH)

    pl.semaphore_signal(barrier, inc=1, device_id={"exc": 1 - core}, device_id_type=MESH)

    loads = []
    for source, target in (
        (perm_hbm.at[0], perm), (mode_hbm, mode_v), (e_hbm.at[:, 0], e), (h_hbm.at[:, 0], h), (inv_hbm, inverse),
        (fwd_hbm.at[:, :, 0], fwd), (mask_hbm.at[0], mask),
    ):
        copy = pltpu.make_async_copy(source, target, load_sem.at[len(loads)])
        copy.start()
        loads.append(copy)

    lane = lax.broadcasted_iota(jnp.int32, (1, LANES), 1)
    low = lane < strip

    loads[0].wait()
    twice = jnp.concatenate([perm[...], perm[...]], 0)
    eps_t[...] = twice.T
    for block in range(n):
        first = eps_t[block * strip : block * strip + strip // 2, :]
        second = eps_t[block * strip + strip // 2 : (block + 1) * strip, :]
        p_send[block] = jnp.where(low, first, second)
    r_first[0:cells, :] = COURANT * (1.0 / eps_t[...])
    r_first[cells:, :] = jnp.zeros((PAD, LANES), F32)

    loads[1].wait()
    for block in range(cells // LANES):
        line = jnp.broadcast_to(mode_v[block : block + 1, :], (LANES, LANES))
        mode_col[block * LANES : (block + 1) * LANES, :] = line.T
    mode_col[cells:, :] = jnp.zeros((PAD, LANES), F32)
    amplitudes = [jnp.cos(jnp.full((1, LANES), omega[0] * (s + 1), F32)) for s in range(2)]
    at_plane = plane[0]

    loads[2].wait()
    loads[3].wait()
    halo[...] = jnp.concatenate(
        [
            e[0, 0:1, :], e[2, 0:1, :], h[0, 0:1, :], h[2, 0:1, :], perm[0:1, :],
            h[0, strip - 1 : strip, :], h[2, strip - 1 : strip, :], perm[0:1, :],
        ],
        0,
    )

    pl.semaphore_wait(barrier, n)

    to_above = pltpu.make_async_remote_copy(
        halo, halo_lo, halo_send_sem.at[0], halo_recv_sem.at[0], device_id={"line": above}, device_id_type=MESH
    )
    to_below = pltpu.make_async_remote_copy(
        halo, halo_hi, halo_send_sem.at[1], halo_recv_sem.at[1], device_id={"line": below}, device_id_type=MESH
    )
    to_above.start()
    to_below.start()

    def p_copy(to, slot):
        return pltpu.make_async_remote_copy(
            p_send.at[to, pl.ds(pl.multiple_of(core * half, half), half)], p_recv.at[core, slot], p_send_sem.at[to], p_recv_sem.at[slot],
            device_id={"line": to}, device_id_type=MESH,
        )

    for other in others:
        p_copy(other, me).start()
    p_recv[core, me] = p_send[me, pl.ds(pl.multiple_of(core * half, half), half), :]

    to_above.wait()
    to_below.wait()
    is_first, is_last = (me == 0, me == n - 1)
    x_at = lax.broadcasted_iota(jnp.int32, (1, cells), 1)
    column = jnp.where(x_at == at_plane, 1.0, 0.0)
    profile = mode_col[pl.ds(pl.multiple_of(me * strip, strip), strip + PAD), :] * amplitudes[0]
    profile = jnp.concatenate([profile] * (cells // LANES), 1)
    source = profile * column
    r = COURANT * (1.0 / perm[...])
    ex, ez, hx, hz = (e[0], e[2] + source[0:strip], h[0], h[2])
    hx_lo = jnp.where(is_first, 0.0, halo_lo[5:6, :])
    hz_lo = jnp.where(is_first, 0.0, halo_lo[6:7, :])
    ex = ex + r * (hz - shifted_down(hz, hz_lo))
    ez = ez - r * (hx - shifted_down(hx, hx_lo))
    r_hi = COURANT * (1.0 / halo_hi[4:5, :])
    ex_hi = halo_hi[0:1, :] + r_hi * (halo_hi[3:4, :] - hz[strip - 1 : strip])
    ez_hi = halo_hi[1:2, :] + source[strip : strip + 1] - r_hi * (halo_hi[2:3, :] - hx[strip - 1 : strip])
    ex_hi = jnp.where(is_last, 0.0, ex_hi)
    ez_hi = jnp.where(is_last, 0.0, ez_hi)
    hx = hx - COURANT * (shifted_up(ez, ez_hi) - ez)
    hz = hz + COURANT * (shifted_up(ex, ex_hi) - ex)
    for at, value in enumerate((ex, ez, h[1], e[1], hz, hx)):
        lines[at * strip : (at + 1) * strip, :] = value.astype(BF16)

    groups = ((0, 2), (2, 1), (3, 1), (4, 1), (5, 1), (6, 1), (7, 2))

    def copy_out(group, to, slot):
        first, count = groups[group]
        if count == 2:
            out, into = (send_two.at[first // 7, to], recv_two.at[first // 7, slot])
        else:
            out, into = (send.at[first - 2, to], recv.at[first - 2, slot])
        return pltpu.make_async_remote_copy(
            out, into, send_sem.at[group, to], recv_sem.at[group, slot],
            device_id={"line": to}, device_id_type=MESH,
        )

    def tile_at(tile, one, two, device):
        if 2 <= tile <= 6:
            return one.at[tile - 2, device]
        return two.at[tile // 7, device, (tile - 7 if tile >= 7 else tile)]

    def send_all(group):
        for other in others:
            copy_out(group, other, me).start()
        keep_own(group)

    def keep_own(group):
        first, count = groups[group]
        for tile in range(first, first + count):
            tile_at(tile, recv, recv_two, me)[...] = tile_at(tile, send, send_two, me)[...]

    def receive_all(group):
        def take(k, carry):
            other = lax.rem(me + k, n)
            copy_out(group, other, other).wait_recv()
            return carry

        lax.fori_loop(1, n, take, 0)

    def assemble(message, tile):
        at = tile * LANES
        for k in range(n // 2):
            a, b = [tile_at(message, recv, recv_two, 2 * k + odd)[...] for odd in range(2)]
            cut = slice(k * LANES, (k + 1) * LANES)
            lines[at : at + strip, cut] = jnp.concatenate([a[:, :strip], b[:, :strip]], 1)
            lines[at + strip : at + LANES, cut] = jnp.concatenate([a[:, strip:], b[:, strip:]], 1)

    def solve_tile(tile):
        part = lines[tile * LANES : (tile + 1) * LANES, :]
        solved[tile, PAD : cells + PAD, :] = contract(inverse[...], part)

    rows = LANES

    def put(message, device, tile):
        for part in range(rows // strip):
            target = tile_at(message, send, send_two, device + part)
            target[...] = tile[part * strip : (part + 1) * strip].astype(BF16)

    def swap(tile):
        return pltpu.roll(tile, LANES // 2, 1)

    def extended(tile, off, back):
        return solved[tile, off - back : off - back + rows + PAD, :]

    def next_row(value):
        return pltpu.roll(value, value.shape[0] - 1, 0)

    def in_grid(start):
        return lax.broadcasted_iota(jnp.int32, (rows + PAD, LANES), 0) + start < cells

    def curl_x_first(off, at, count):
        b, bd = (solved[1, off : off + count, :], solved[1, off - 1 : off - 1 + count, :])
        hy, hyd = (jnp.where(low, b, swap(b)), jnp.where(low, bd, swap(bd)))
        a = solved[0, off : off + count, :] + r_first[pl.ds(at, count), :] * jnp.where(low, -hy, hy - hyd)
        solved[0, off : off + count, :] = a
        return a

    def curl_x_second(off, at):
        a, b, c = (extended(0, off, 0), extended(1, off, 0), extended(2, off, 0))
        sa, sc = (swap(a), swap(c))
        dc = sc - swap(extended(2, off, 1))
        ey = b + r_first[pl.ds(at, rows + PAD), :] * (c - dc)
        ey = jnp.where(in_grid(at), ey, 0.0)
        hy = b + COURANT * ((next_row(sa) - sa) + a)
        sy = swap(ey)
        c = c - COURANT * jnp.where(low, next_row(sy) - sy, ey)
        return jnp.where(low, hy, ey)[0:rows], c[0:rows]

    def curl_y(tile, start, sign, source):
        t, td = (extended(tile, start + PAD, 0), extended(tile, start + PAD, 1))
        st, std = (swap(t), swap(td))
        p = t if source is None else t + source
        p = p + sign * r_second[start : start + rows + PAD, :] * (st - std)
        p = jnp.where(in_grid(start), p, 0.0)
        sp = swap(p)
        q = t + sign * COURANT * (next_row(sp) - sp)
        return jnp.where(low, p, q)[0:rows]

    def along(electric, instant):
        return (
            electric[0] * fwd[instant, 0].astype(F32)
            + electric[1] * fwd[instant, 1].astype(F32)
            + electric[2] * fwd[instant, 2].astype(F32)
        )

    starts = range(0, cells, rows)

    loads[4].wait()
    inv[0:EDGE, :] = jnp.zeros((EDGE, cells), BF16)
    inv[cells + EDGE :, :] = jnp.zeros((EDGE, cells), BF16)
    quarter, group = (cells // 4, n // 4)
    for turn in (2, 3, 1, 0):
        plane_of = lax.rem(me // group + turn, 4)
        at = pl.multiple_of(plane_of * quarter, quarter)
        result = contract(inv[pl.ds(at, quarter + 2 * EDGE), :], lines[...])
        for tile in range(3):
            solved[tile, 0 : quarter + 2 * EDGE, :] = result[:, tile * LANES : (tile + 1) * LANES]
        for part in range(0, quarter, rows):
            curl_x_first(EDGE + part, pl.multiple_of(at + part, rows), rows)
        curl_x_first(EDGE + quarter, pl.multiple_of(at + quarter, rows), PAD)
        for part in range(0, quarter, rows):
            b, c = curl_x_second(EDGE + part, pl.multiple_of(at + part, rows))
            a = solved[0, EDGE + part : EDGE + part + rows, :]
            device = plane_of * group + part // strip
            put(0, device, jnp.where(low, a, swap(c)))
            put(1, device, jnp.where(low, swap(a), c))
            put(2, device, b)
        for k in range(1 if turn == 0 else 0, group):
            other = plane_of * group + lax.rem(lax.rem(me, group) + k, group)
            copy_out(0, other, me).start()
    keep_own(0)
    send_all(1)

    for tile in range(3):
        solved[tile, 0:PAD, :] = jnp.zeros((PAD, LANES), F32)
        solved[tile, cells + PAD :, :] = jnp.zeros((PAD, LANES), F32)

    def p_take(k, carry):
        other = lax.rem(me + k, n)
        p_copy(other, other).wait_recv()
        return carry

    lax.fori_loop(1, n, p_take, 0)
    hand_over = pltpu.make_async_remote_copy(
        p_recv.at[core], p_recv.at[core], hand_sem.at[0], hand_sem.at[1],
        device_id={"exc": 1 - core}, device_id_type=MESH,
    )
    hand_over.start()
    hand_over.wait()
    for k in range(n // 2):
        cut = slice(k * LANES, (k + 1) * LANES)
        for part in range(2):
            a, b = (p_recv[part, 2 * k], p_recv[part, 2 * k + 1])
            one, two = (part * half, part * half + strip // 2)
            inv_eps[one : one + half, cut] = 1.0 / jnp.concatenate([a[:, :strip], b[:, :strip]], 1)
            inv_eps[two : two + half, cut] = 1.0 / jnp.concatenate([a[:, strip:], b[:, strip:]], 1)
    both = jnp.concatenate([inv_eps[...], inv_eps[...]], 0)
    r_second[0:cells, :] = COURANT * both.T
    r_second[cells:, :] = jnp.zeros((PAD, LANES), F32)
    loads[5].wait()
    loads[6].wait()

    receive_all(0)
    assemble(0, 0)
    solve_tile(0)
    for start in starts:
        kept[start : start + rows, :] = curl_y(0, start, 1.0, None)
    assemble(1, 1)
    solve_tile(1)
    here = jnp.where(low & (lane + me * strip == at_plane), 1.0, 0.0)
    for start in starts:
        source = (amplitudes[1] * mode_col[start : start + rows + PAD, :]) * here
        b = curl_y(1, start, -1.0, source)
        a = kept[start : start + rows, :]
        put(3, start // strip, jnp.where(low, a, swap(b)))
        put(5, start // strip, jnp.where(low, swap(a), b))
    send_all(2)
    receive_all(1)
    assemble(2, 2)
    solve_tile(2)
    for start in starts:
        put(4, start // strip, solved[2, start + PAD : start + PAD + rows, :])
    send_all(3)
    send_all(4)

    weight = mask[...].astype(F32)
    square = inv_eps[...] * inv_eps[...]
    electric = jnp.concatenate(
        [lines[0:strip, :], lines[LANES + strip * 0 : LANES + strip, :], lines[2 * LANES + strip :, :]], 0
    )
    electric = contract(electric, inverse[...])
    parts = (electric[0:strip], electric[2 * strip :], electric[strip : 2 * strip])
    grad[...] = weight * along(parts, 0) * square

    for tile in range(2):
        receive_all(2 + tile)
        assemble(3 + tile, tile)
        solve_tile(tile)
    for start in starts:
        put(6, start // strip, curl_x_first(start + PAD, start, rows))
    send_all(5)
    receive_all(4)
    assemble(5, 2)
    solve_tile(2)
    for start in starts:
        b, c = curl_x_second(start + PAD, start)
        put(7, start // strip, b)
        put(8, start // strip, c)
    send_all(6)

    receive_all(5)
    assemble(6, 0)
    pair = contract(lines[0:LANES, :], inverse[...])
    oe[0, 0] = pair[:strip]
    oe[2, 0] = pair[strip:]
    receive_all(6)
    assemble(7, 1)
    pair = contract(lines[LANES : 2 * LANES, :], inverse[...])
    oh[1, 0] = pair[:strip]
    oe[1, 0] = pair[strip:]
    og[0] = grad[...] + weight * along((oe[0, 0], pair[strip:], oe[2, 0]), 1) * square
    assemble(8, 2)
    pair = contract(lines[2 * LANES :, :], inverse[...])
    oh[2, 0] = pair[:strip]
    oh[0, 0] = pair[strip:]

    def settle(k, carry):
        other = lax.rem(me + k, n)
        p_copy(other, other).wait_send()
        for group in range(len(groups)):
            copy_out(group, other, other).wait_send()
        return carry

    lax.fori_loop(1, n, settle, 0)


def write_out(e, h, g, oe, oh, og, sem):
    copies = []
    for source, target in ((e, oe), (h, oh)):
        for at in range(3):
            copies.append(pltpu.make_async_copy(source.at[at], target.at[at], sem.at[len(copies)]))
    copies.append(pltpu.make_async_copy(g, og, sem.at[len(copies)]))
    for copy in copies:
        copy.start()
    for copy in copies:
        copy.wait()


def fused(adj_e, adj_h, fwd_e, permittivity, design_mask, inverse, omega, port_mode, port_plane):
    n = lax.axis_size("line")
    cells, strip = (inverse.shape[0], adj_e.shape[2])
    steps = fwd_e.shape[0]
    hbm = pl.BlockSpec(memory_space=pltpu.HBM)
    vmem = pl.BlockSpec(memory_space=pltpu.VMEM)
    smem = pl.BlockSpec(memory_space=pltpu.SMEM)
    scratch = [
        pltpu.VMEM((3, strip, cells), F32),
        pltpu.VMEM((3, strip, cells), F32),
        pltpu.VMEM((steps, 3, strip, cells), BF16),
        pltpu.VMEM((strip, cells), F32),
        pltpu.VMEM((strip, cells), jnp.int32),
        pltpu.VMEM((cells + 2 * EDGE, cells), BF16),
        pltpu.VMEM((8, cells), F32),
        pltpu.VMEM((8, cells), F32),
        pltpu.VMEM((8, cells), F32),
        pltpu.VMEM((n, strip // 2, LANES), F32),
        pltpu.VMEM((2, n, strip // 4, LANES), F32),
        pltpu.VMEM((cells, LANES), F32),
        pltpu.VMEM((cells + PAD, LANES), F32),
        pltpu.VMEM((cells + PAD, LANES), F32),
        pltpu.VMEM((strip, cells), F32),
        pltpu.VMEM((cells // LANES, LANES), F32),
        pltpu.VMEM((cells + PAD, LANES), F32),
        pltpu.VMEM((6 * strip, cells), BF16),
        pltpu.VMEM((3, cells + 2 * PAD, LANES), F32),
        pltpu.VMEM((cells, LANES), F32),
        pltpu.VMEM((5, n, strip, LANES), BF16),
        pltpu.VMEM((5, n, strip, LANES), BF16),
        pltpu.VMEM((2, n, 2, strip, LANES), BF16),
        pltpu.VMEM((2, n, 2, strip, LANES), BF16),
        pltpu.VMEM((strip, cells), F32),
        pltpu.SemaphoreType.DMA((7,)),
        pltpu.SemaphoreType.DMA((2,)),
        pltpu.SemaphoreType.DMA((2,)),
        pltpu.SemaphoreType.DMA((2,)),
        pltpu.SemaphoreType.DMA((n,)),
        pltpu.SemaphoreType.DMA((n,)),
        pltpu.SemaphoreType.DMA((7, n)),
        pltpu.SemaphoreType.DMA((7, n)),
    ]
    shapes = tuple(jax.ShapeDtypeStruct(a.shape, F32) for a in (adj_e, adj_h, permittivity))
    results = pl.pallas_call(
        functools.partial(kernel, n),
        out_shape=tuple(pltpu.VMEM(a.shape, F32) for a in shapes),
        in_specs=[hbm] * 6 + [smem, hbm, smem],
        out_specs=(vmem, vmem, vmem),
        scratch_shapes=scratch,
        compiler_params=pltpu.CompilerParams(
            collective_id=0, has_side_effects=True, vmem_limit_bytes=60 * 1024 * 1024
        ),
    )(
        adj_e, adj_h, fwd_e, permittivity, design_mask, inverse, omega,
        port_mode.reshape(cells // LANES, LANES), port_plane,
    )
    return tuple(
        pl.pallas_call(
            write_out,
            out_shape=shapes,
            in_specs=[pl.BlockSpec(memory_space=pl.ANY)] * 3,
            out_specs=(hbm, hbm, hbm),
            scratch_shapes=[pltpu.SemaphoreType.DMA((7,))],
            compiler_params=pltpu.CompilerParams(vmem_limit_bytes=1024 * 1024),
        )(*results)
    )


def per_device(adj_e, adj_h, fwd_e, permittivity, design_mask, inverse, omega, port_mode, port_plane):
    args = (adj_e, adj_h, fwd_e, permittivity, design_mask, inverse, omega, port_mode, port_plane)
    paired = 2 * adj_e.shape[2] == LANES and fwd_e.shape[0] == 2 and lax.axis_size("exc") == 2 and permittivity.shape[0] == 1
    return fused(*args) if paired else plain_per_device(*args)


def solution(mesh):
    in_specs = (
        P(None, "exc", "line", None),
        P(None, "exc", "line", None),
        P(None, None, "exc", "line", None),
        P(None, "line", None),
        P(None, "line", None),
        P(),
        P("exc"),
        P("exc"),
        P("exc"),
    )
    out_specs = (P(None, "exc", "line", None), P(None, "exc", "line", None), P("exc", "line", None))
    return jax.shard_map(
        per_device, mesh=mesh, in_specs=in_specs, out_specs=out_specs, check_vma=False
    )
```

```python
import functools

import jax
import jax.numpy as jnp
from jax import lax
from jax.experimental import pallas as pl
from jax.experimental.pallas import tpu as pltpu
from jax.sharding import PartitionSpec as P

COURANT = 0.4


def extended(array, sides, width):
    for axis, dim in sides:
        devices, length = (lax.axis_size(axis), array.shape[dim])
        up = [(i, (i + 1) % devices) for i in range(devices - 1)]
        down = [(j, i) for i, j in up]
        last = lax.slice_in_dim(array, length - width, length, axis=dim)
        first = lax.slice_in_dim(array, 0, width, axis=dim)
        before = lax.ppermute(last, axis, up)
        after = lax.ppermute(first, axis, down)
        array = jnp.concatenate([before, array, after], axis=dim)
    return array


def lower_diff(padded, along):
    inner = padded.shape[along] - 2
    middle = lax.slice_in_dim(padded, 1, inner + 1, axis=along)
    return middle - lax.slice_in_dim(padded, 0, inner, axis=along)


def upper_diff(padded, along):
    inner = padded.shape[along] - 2
    middle = lax.slice_in_dim(padded, 1, inner + 1, axis=along)
    return lax.slice_in_dim(padded, 2, inner + 2, axis=along) - middle


def zero_rim(stacked, along):
    widths = [(0, 0)] * stacked.ndim
    widths[along] = (1, 1)
    return jnp.pad(stacked, widths)


def row_rim(stacked, along):
    return extended(stacked, (("line", 2),), 1)


def column_rim(stacked, along):
    return extended(stacked, (("line", 2),), 1)


def curl_along_y(fields, inverse_eps, extend, along):
    electric_x, electric_y, electric_z = (fields[0], fields[1], fields[2])
    magnetic_x, magnetic_y, magnetic_z = (fields[3], fields[4], fields[5])
    scaled = COURANT * inverse_eps
    lower_terms = lower_diff(extend(jnp.stack([magnetic_x, magnetic_z]), along), along)
    electric_x = electric_x + scaled * lower_terms[1]
    electric_z = electric_z - scaled * lower_terms[0]
    upper_terms = upper_diff(extend(jnp.stack([electric_x, electric_z]), along), along)
    magnetic_x = magnetic_x - COURANT * upper_terms[1]
    magnetic_z = magnetic_z + COURANT * upper_terms[0]
    return jnp.stack([electric_x, electric_y, electric_z, magnetic_x, magnetic_y, magnetic_z])


def curl_along_xz(fields, inverse_eps, extend, along):
    electric_x, electric_y, electric_z = (fields[0], fields[1], fields[2])
    magnetic_x, magnetic_y, magnetic_z = (fields[3], fields[4], fields[5])
    scaled = COURANT * inverse_eps
    depth_terms = lower_diff(zero_rim(jnp.stack([magnetic_x, magnetic_y]), 1), 1)
    across = lower_diff(extend(jnp.stack([magnetic_y, magnetic_z]), along), along)
    electric_x = electric_x - scaled * depth_terms[1]
    electric_y = electric_y + scaled * (depth_terms[0] - across[1])
    electric_z = electric_z + scaled * across[0]
    depth_upper = upper_diff(zero_rim(jnp.stack([electric_x, electric_y]), 1), 1)
    across_upper = upper_diff(extend(jnp.stack([electric_y, electric_z]), along), along)
    magnetic_x = magnetic_x + COURANT * depth_upper[1]
    magnetic_y = magnetic_y + COURANT * (across_upper[1] - depth_upper[0])
    magnetic_z = magnetic_z - COURANT * across_upper[0]
    return jnp.stack([electric_x, electric_y, electric_z, magnetic_x, magnetic_y, magnetic_z])


def line_solve(rounded, inverse):
    flattened = rounded.reshape(-1, rounded.shape[-1])
    solved = lax.dot_general(
        flattened, inverse, (((1,), (1,)), ((), ())), preferred_element_type=jnp.float32
    )
    return solved.reshape(rounded.shape)


def fold_lines(field, line_count):
    strip_width = field.shape[-2]
    block = field.shape[-1] // line_count
    regrouped = field.reshape(field.shape[:-2] + (strip_width, line_count, block))
    regrouped = jnp.moveaxis(regrouped, -3, -1)
    return regrouped.reshape(field.shape[:-2] + (line_count, block * strip_width))


def unfold(received, block):
    line_count = received.shape[-2]
    strip_width = received.shape[-1] // block
    regrouped = received.reshape(received.shape[:-2] + (line_count, block, strip_width))
    regrouped = jnp.moveaxis(regrouped, -3, -2)
    return regrouped.reshape(received.shape[:-2] + (block, line_count * strip_width))


def accumulate(gradient, fields, snapshot, mask_weight, inverse_cols):
    forward = snapshot.astype(jnp.float32)
    intersection = fields[0] * forward[0] + fields[1] * forward[1] + fields[2] * forward[2]
    return gradient + mask_weight * intersection * (inverse_cols * inverse_cols)


def plain_per_device(
    adj_e, adj_h, fwd_e, permittivity, design_mask, inverse, omega, port_mode, port_plane
):
    line_cells = inverse.shape[0]
    strip_width = adj_e.shape[2]
    step_count = fwd_e.shape[0]
    line_count = lax.axis_size("line")
    fields = jnp.concatenate([adj_e, adj_h], 0)
    inverse_rows = 1.0 / permittivity
    eps_turned = lax.all_to_all(
        fold_lines(permittivity, line_count), "line", split_axis=1, concat_axis=1, tiled=True
    )
    inverse_cols = 1.0 / unfold(eps_turned, strip_width)
    frequency = omega[0]
    plane_at = port_plane[0]
    offset = lax.axis_index("line") * strip_width
    column = (jnp.arange(line_cells, dtype=jnp.int32) == plane_at).astype(jnp.float32)
    profile_rows = lax.dynamic_slice_in_dim(port_mode, offset, strip_width)
    mask_weight = design_mask.astype(jnp.float32)
    gradient = jnp.zeros(permittivity.shape, jnp.float32)
    for instant in range(step_count):
        amplitude = jnp.cos(frequency * (instant + 1))
        fields = fields.at[2].add(amplitude * profile_rows[None, :, None] * column[None, None, :])
        fields = curl_along_y(fields, inverse_rows, row_rim, 2)
        fields = line_solve(fields.astype(jnp.bfloat16), inverse)
        turned = unfold(
            lax.all_to_all(
                fold_lines(fields, line_count), "line", split_axis=2, concat_axis=2, tiled=True
            ),
            strip_width,
        )
        turned = curl_along_xz(turned, inverse_cols, column_rim, 2)
        turned = line_solve(turned.astype(jnp.bfloat16), inverse)
        gradient = accumulate(gradient, turned, fwd_e[instant], mask_weight, inverse_cols)
        if instant + 1 < step_count:
            fields = unfold(
                lax.all_to_all(
                    fold_lines(turned, line_count), "line", split_axis=2, concat_axis=2, tiled=True
                ),
                strip_width,
            )
    return (turned[:3], turned[3:], gradient)


LANES = 128
MESH = pl.DeviceIdType.MESH
PAD = 8
EDGE = 16
F32, BF16 = (jnp.float32, jnp.bfloat16)


def contract(left, right):
    return lax.dot_general(left, right, (((1,), (1,)), ((), ())), preferred_element_type=F32)


def shifted_down(value, first):
    row = lax.broadcasted_iota(jnp.int32, value.shape, 0)
    return jnp.where(row == 0, first, pltpu.roll(value, 1, 0))


def shifted_up(value, last):
    rows = value.shape[0]
    row = lax.broadcasted_iota(jnp.int32, value.shape, 0)
    return jnp.where(row == rows - 1, last, pltpu.roll(value, rows - 1, 0))


def kernel(
    n, e_hbm, h_hbm, fwd_hbm, perm_hbm, mask_hbm, inv_hbm, omega, mode_hbm, plane,
    oe, oh, og,
    e, h, fwd, perm, mask, inv, halo, halo_lo, halo_hi, p_send, p_recv, eps_t, r_first, r_second, inv_eps,
    mode_v, mode_col, lines, solved, kept, send, recv, send_two, recv_two, grad,
    load_sem, hand_sem, halo_send_sem, halo_recv_sem, p_send_sem, p_recv_sem, send_sem, recv_sem,
):
    me, core = (lax.axis_index("line"), lax.axis_index("exc"))
    strip = perm.shape[0]
    cells = perm.shape[1]
    half = strip // 4
    inverse = inv.at[EDGE : cells + EDGE]
    above, below = (lax.rem(me + 1, n), lax.rem(me + n - 1, n))

    barrier = pltpu.get_barrier_semaphore()

    far = sorted(range(1, n), key=lambda k: -min(k, n - k))
    turns = [k for two in zip(far, far[::-1]) for k in two][: n - 1]
    others = [lax.rem(me + k, n) for k in turns]
    for other in others:
        pl.semaphore_signal(barrier, inc=1, device_id={"line": other}, device_id_type=MESH)

    pl.semaphore_signal(barrier, inc=1, device_id={"exc": 1 - core}, device_id_type=MESH)

    loads = []
    for source, target in (
        (e_hbm.at[:, 0], e), (h_hbm.at[:, 0], h), (perm_hbm.at[0], perm), (mode_hbm, mode_v), (inv_hbm, inverse),
        (fwd_hbm.at[:, :, 0], fwd), (mask_hbm.at[0], mask),
    ):
        copy = pltpu.make_async_copy(source, target, load_sem.at[len(loads)])
        copy.start()
        loads.append(copy)

    lane = lax.broadcasted_iota(jnp.int32, (1, LANES), 1)
    low = lane < strip

    for load in loads[:3]:
        load.wait()
    halo[...] = jnp.concatenate(
        [
            e[0, 0:1, :], e[2, 0:1, :], h[0, 0:1, :], h[2, 0:1, :], perm[0:1, :],
            h[0, strip - 1 : strip, :], h[2, strip - 1 : strip, :], perm[0:1, :],
        ],
        0,
    )

    pl.semaphore_wait(barrier, n)

    to_above = pltpu.make_async_remote_copy(
        halo, halo_lo, halo_send_sem.at[0], halo_recv_sem.at[0], device_id={"line": above}, device_id_type=MESH
    )
    to_below = pltpu.make_async_remote_copy(
        halo, halo_hi, halo_send_sem.at[1], halo_recv_sem.at[1], device_id={"line": below}, device_id_type=MESH
    )
    to_above.start()
    to_below.start()

    twice = jnp.concatenate([perm[...], perm[...]], 0)
    eps_t[...] = twice.T
    for block in range(n):
        first = eps_t[block * strip : block * strip + strip // 2, :]
        second = eps_t[block * strip + strip // 2 : (block + 1) * strip, :]
        p_send[block] = jnp.where(low, first, second)
    def p_copy(to, slot):
        return pltpu.make_async_remote_copy(
            p_send.at[to, pl.ds(pl.multiple_of(core * half, half), half)], p_recv.at[core, slot], p_send_sem.at[to], p_recv_sem.at[slot],
            device_id={"line": to}, device_id_type=MESH,
        )

    for other in others:
        p_copy(other, me).start()
    p_recv[core, me] = p_send[me, pl.ds(pl.multiple_of(core * half, half), half), :]

    r_first[0:cells, :] = COURANT * (1.0 / eps_t[...])
    r_first[cells:, :] = jnp.zeros((PAD, LANES), F32)

    loads[3].wait()
    for block in range(cells // LANES):
        line = jnp.broadcast_to(mode_v[block : block + 1, :], (LANES, LANES))
        mode_col[block * LANES : (block + 1) * LANES, :] = line.T
    mode_col[cells:, :] = jnp.zeros((PAD, LANES), F32)
    amplitudes = [jnp.cos(jnp.full((1, LANES), omega[0] * (s + 1), F32)) for s in range(2)]
    at_plane = plane[0]

    is_first, is_last = (me == 0, me == n - 1)
    x_at = lax.broadcasted_iota(jnp.int32, (1, cells), 1)
    column = jnp.where(x_at == at_plane, 1.0, 0.0)
    profile = mode_col[pl.ds(pl.multiple_of(me * strip, strip), strip + PAD), :] * amplitudes[0]
    profile = jnp.concatenate([profile] * (cells // LANES), 1)
    source = profile * column
    r = COURANT * (1.0 / perm[...])
    ex, ez, hx, hz = (e[0], e[2] + source[0:strip], h[0], h[2])
    to_above.wait()
    to_below.wait()
    hx_lo = jnp.where(is_first, 0.0, halo_lo[5:6, :])
    hz_lo = jnp.where(is_first, 0.0, halo_lo[6:7, :])
    ex = ex + r * (hz - shifted_down(hz, hz_lo))
    ez = ez - r * (hx - shifted_down(hx, hx_lo))
    r_hi = COURANT * (1.0 / halo_hi[4:5, :])
    ex_hi = halo_hi[0:1, :] + r_hi * (halo_hi[3:4, :] - hz[strip - 1 : strip])
    ez_hi = halo_hi[1:2, :] + source[strip : strip + 1] - r_hi * (halo_hi[2:3, :] - hx[strip - 1 : strip])
    ex_hi = jnp.where(is_last, 0.0, ex_hi)
    ez_hi = jnp.where(is_last, 0.0, ez_hi)
    hx = hx - COURANT * (shifted_up(ez, ez_hi) - ez)
    hz = hz + COURANT * (shifted_up(ex, ex_hi) - ex)
    for at, value in enumerate((ex, ez, h[1], e[1], hz, hx)):
        lines[at * strip : (at + 1) * strip, :] = value.astype(BF16)

    groups = ((0, 2), (2, 1), (3, 1), (4, 1), (5, 1), (6, 1), (7, 1), (8, 1))

    def copy_out(group, to, slot):
        first, count = groups[group]
        if count == 2:
            out, into = (send_two.at[to], recv_two.at[slot])
        else:
            out, into = (send.at[first - 2, to], recv.at[first - 2, slot])
        return pltpu.make_async_remote_copy(
            out, into, send_sem.at[group, to], recv_sem.at[group, slot],
            device_id={"line": to}, device_id_type=MESH,
        )

    def tile_at(tile, one, two, device):
        return two.at[device, tile] if tile < 2 else one.at[tile - 2, device]

    def send_all(group):
        for other in others:
            copy_out(group, other, me).start()
        keep_own(group)

    def keep_own(group):
        first, count = groups[group]
        for tile in range(first, first + count):
            tile_at(tile, recv, recv_two, me)[...] = tile_at(tile, send, send_two, me)[...]

    def receive_all(group):
        def take(k, carry):
            other = lax.rem(me + k, n)
            copy_out(group, other, other).wait_recv()
            return carry

        lax.fori_loop(1, n, take, 0)

    def assemble(message, tile):
        at = tile * LANES
        for k in range(n // 2):
            a, b = [tile_at(message, recv, recv_two, 2 * k + odd)[...] for odd in range(2)]
            cut = slice(k * LANES, (k + 1) * LANES)
            lines[at : at + strip, cut] = jnp.concatenate([a[:, :strip], b[:, :strip]], 1)
            lines[at + strip : at + LANES, cut] = jnp.concatenate([a[:, strip:], b[:, strip:]], 1)

    def solve_tile(tile):
        part = lines[tile * LANES : (tile + 1) * LANES, :]
        solved[tile, PAD : cells + PAD, :] = contract(inverse[...], part)

    rows = LANES

    def put(message, device, tile):
        for part in range(rows // strip):
            target = tile_at(message, send, send_two, device + part)
            target[...] = tile[part * strip : (part + 1) * strip].astype(BF16)

    def swap(tile):
        return pltpu.roll(tile, LANES // 2, 1)

    def extended(tile, off, back):
        return solved[tile, off - back : off - back + rows + PAD, :]

    def next_row(value):
        return pltpu.roll(value, value.shape[0] - 1, 0)

    def in_grid(start):
        return lax.broadcasted_iota(jnp.int32, (rows + PAD, LANES), 0) + start < cells

    def curl_x_first(off, at, count):
        b, bd = (solved[1, off : off + count, :], solved[1, off - 1 : off - 1 + count, :])
        hy, hyd = (jnp.where(low, b, swap(b)), jnp.where(low, bd, swap(bd)))
        a = solved[0, off : off + count, :] + r_first[pl.ds(at, count), :] * jnp.where(low, -hy, hy - hyd)
        solved[0, off : off + count, :] = a
        return a

    def curl_x_second(off, at):
        a, b, c = (extended(0, off, 0), extended(1, off, 0), extended(2, off, 0))
        sa, sc = (swap(a), swap(c))
        dc = sc - swap(extended(2, off, 1))
        ey = b + r_first[pl.ds(at, rows + PAD), :] * (c - dc)
        ey = jnp.where(in_grid(at), ey, 0.0)
        hy = b + COURANT * ((next_row(sa) - sa) + a)
        sy = swap(ey)
        c = c - COURANT * jnp.where(low, next_row(sy) - sy, ey)
        return jnp.where(low, hy, ey)[0:rows], c[0:rows]

    def curl_y(tile, start, sign, source):
        t, td = (extended(tile, start + PAD, 0), extended(tile, start + PAD, 1))
        st, std = (swap(t), swap(td))
        p = t if source is None else t + source
        p = p + sign * r_second[start : start + rows + PAD, :] * (st - std)
        p = jnp.where(in_grid(start), p, 0.0)
        sp = swap(p)
        q = t + sign * COURANT * (next_row(sp) - sp)
        return jnp.where(low, p, q)[0:rows]

    def along(electric, instant):
        return (
            electric[0] * fwd[instant, 0].astype(F32)
            + electric[1] * fwd[instant, 1].astype(F32)
            + electric[2] * fwd[instant, 2].astype(F32)
        )

    starts = range(0, cells, rows)

    loads[4].wait()
    inv[0:EDGE, :] = jnp.zeros((EDGE, cells), BF16)
    inv[cells + EDGE :, :] = jnp.zeros((EDGE, cells), BF16)
    quarter, group = (cells // 4, n // 4)
    for turn in (2, 3, 1, 0):
        plane_of = lax.rem(me // group + turn, 4)
        at = pl.multiple_of(plane_of * quarter, quarter)
        result = contract(inv[pl.ds(at, quarter + 2 * EDGE), :], lines[...])
        for tile in range(3):
            solved[tile, 0 : quarter + 2 * EDGE, :] = result[:, tile * LANES : (tile + 1) * LANES]
        for part in range(0, quarter, rows):
            curl_x_first(EDGE + part, pl.multiple_of(at + part, rows), rows)
        curl_x_first(EDGE + quarter, pl.multiple_of(at + quarter, rows), PAD)
        for part in range(0, quarter, rows):
            b, c = curl_x_second(EDGE + part, pl.multiple_of(at + part, rows))
            a = solved[0, EDGE + part : EDGE + part + rows, :]
            device = plane_of * group + part // strip
            put(0, device, jnp.where(low, a, swap(c)))
            put(1, device, jnp.where(low, swap(a), c))
            put(2, device, b)
        for k in range(1 if turn == 0 else 0, group):
            other = plane_of * group + lax.rem(lax.rem(me, group) + k, group)
            copy_out(0, other, me).start()
    keep_own(0)
    send_all(1)

    for tile in range(3):
        solved[tile, 0:PAD, :] = jnp.zeros((PAD, LANES), F32)
        solved[tile, cells + PAD :, :] = jnp.zeros((PAD, LANES), F32)

    def p_take(k, carry):
        other = lax.rem(me + k, n)
        p_copy(other, other).wait_recv()
        return carry

    lax.fori_loop(1, n, p_take, 0)
    hand_over = pltpu.make_async_remote_copy(
        p_recv.at[core], p_recv.at[core], hand_sem.at[0], hand_sem.at[1],
        device_id={"exc": 1 - core}, device_id_type=MESH,
    )
    hand_over.start()
    hand_over.wait()
    for k in range(n // 2):
        cut = slice(k * LANES, (k + 1) * LANES)
        for part in range(2):
            a, b = (p_recv[part, 2 * k], p_recv[part, 2 * k + 1])
            one, two = (part * half, part * half + strip // 2)
            inv_eps[one : one + half, cut] = 1.0 / jnp.concatenate([a[:, :strip], b[:, :strip]], 1)
            inv_eps[two : two + half, cut] = 1.0 / jnp.concatenate([a[:, strip:], b[:, strip:]], 1)
    both = jnp.concatenate([inv_eps[...], inv_eps[...]], 0)
    r_second[0:cells, :] = COURANT * both.T
    r_second[cells:, :] = jnp.zeros((PAD, LANES), F32)
    loads[5].wait()
    loads[6].wait()

    receive_all(0)
    assemble(0, 0)
    solve_tile(0)
    for start in starts:
        kept[start : start + rows, :] = curl_y(0, start, 1.0, None)
    assemble(1, 1)
    solve_tile(1)
    here = jnp.where(low & (lane + me * strip == at_plane), 1.0, 0.0)
    for start in starts:
        source = (amplitudes[1] * mode_col[start : start + rows + PAD, :]) * here
        b = curl_y(1, start, -1.0, source)
        a = kept[start : start + rows, :]
        put(3, start // strip, jnp.where(low, a, swap(b)))
        put(5, start // strip, jnp.where(low, swap(a), b))
    send_all(2)
    receive_all(1)
    assemble(2, 2)
    solve_tile(2)
    for start in starts:
        put(4, start // strip, solved[2, start + PAD : start + PAD + rows, :])
    send_all(3)
    send_all(4)

    weight = mask[...].astype(F32)
    square = inv_eps[...] * inv_eps[...]
    electric = jnp.concatenate(
        [lines[0:strip, :], lines[LANES + strip * 0 : LANES + strip, :], lines[2 * LANES + strip :, :]], 0
    )
    electric = contract(electric, inverse[...])
    parts = (electric[0:strip], electric[2 * strip :], electric[strip : 2 * strip])
    grad[...] = weight * along(parts, 0) * square

    for tile in range(2):
        receive_all(2 + tile)
        assemble(3 + tile, tile)
        solve_tile(tile)
    for start in starts:
        put(6, start // strip, curl_x_first(start + PAD, start, rows))
    send_all(5)
    receive_all(4)
    assemble(5, 2)
    solve_tile(2)
    for start in starts:
        b, c = curl_x_second(start + PAD, start)
        put(7, start // strip, b)
        put(8, start // strip, c)
    send_all(6)
    send_all(7)

    receive_all(5)
    assemble(6, 0)
    pair = contract(lines[0:LANES, :], inverse[...])
    oe[0, 0] = pair[:strip]
    oe[2, 0] = pair[strip:]
    receive_all(6)
    assemble(7, 1)
    pair = contract(lines[LANES : 2 * LANES, :], inverse[...])
    oh[1, 0] = pair[:strip]
    oe[1, 0] = pair[strip:]
    og[0] = grad[...] + weight * along((oe[0, 0], pair[strip:], oe[2, 0]), 1) * square
    receive_all(7)
    assemble(8, 2)
    pair = contract(lines[2 * LANES :, :], inverse[...])
    oh[2, 0] = pair[:strip]
    oh[0, 0] = pair[strip:]

    def settle(k, carry):
        other = lax.rem(me + k, n)
        p_copy(other, other).wait_send()
        for group in range(len(groups)):
            copy_out(group, other, other).wait_send()
        return carry

    lax.fori_loop(1, n, settle, 0)


def write_out(e, h, g, oe, oh, og, sem):
    copies = []
    for source, target in ((e, oe), (h, oh)):
        for at in range(3):
            copies.append(pltpu.make_async_copy(source.at[at], target.at[at], sem.at[len(copies)]))
    copies.append(pltpu.make_async_copy(g, og, sem.at[len(copies)]))
    for copy in copies:
        copy.start()
    for copy in copies:
        copy.wait()


def fused(adj_e, adj_h, fwd_e, permittivity, design_mask, inverse, omega, port_mode, port_plane):
    n = lax.axis_size("line")
    cells, strip = (inverse.shape[0], adj_e.shape[2])
    steps = fwd_e.shape[0]
    hbm = pl.BlockSpec(memory_space=pltpu.HBM)
    vmem = pl.BlockSpec(memory_space=pltpu.VMEM)
    smem = pl.BlockSpec(memory_space=pltpu.SMEM)
    scratch = [
        pltpu.VMEM((3, strip, cells), F32),
        pltpu.VMEM((3, strip, cells), F32),
        pltpu.VMEM((steps, 3, strip, cells), BF16),
        pltpu.VMEM((strip, cells), F32),
        pltpu.VMEM((strip, cells), jnp.int32),
        pltpu.VMEM((cells + 2 * EDGE, cells), BF16),
        pltpu.VMEM((8, cells), F32),
        pltpu.VMEM((8, cells), F32),
        pltpu.VMEM((8, cells), F32),
        pltpu.VMEM((n, strip // 2, LANES), F32),
        pltpu.VMEM((2, n, strip // 4, LANES), F32),
        pltpu.VMEM((cells, LANES), F32),
        pltpu.VMEM((cells + PAD, LANES), F32),
        pltpu.VMEM((cells + PAD, LANES), F32),
        pltpu.VMEM((strip, cells), F32),
        pltpu.VMEM((cells // LANES, LANES), F32),
        pltpu.VMEM((cells + PAD, LANES), F32),
        pltpu.VMEM((6 * strip, cells), BF16),
        pltpu.VMEM((3, cells + 2 * PAD, LANES), F32),
        pltpu.VMEM((cells, LANES), F32),
        pltpu.VMEM((7, n, strip, LANES), BF16),
        pltpu.VMEM((7, n, strip, LANES), BF16),
        pltpu.VMEM((n, 2, strip, LANES), BF16),
        pltpu.VMEM((n, 2, strip, LANES), BF16),
        pltpu.VMEM((strip, cells), F32),
        pltpu.SemaphoreType.DMA((7,)),
        pltpu.SemaphoreType.DMA((2,)),
        pltpu.SemaphoreType.DMA((2,)),
        pltpu.SemaphoreType.DMA((2,)),
        pltpu.SemaphoreType.DMA((n,)),
        pltpu.SemaphoreType.DMA((n,)),
        pltpu.SemaphoreType.DMA((8, n)),
        pltpu.SemaphoreType.DMA((8, n)),
    ]
    shapes = tuple(jax.ShapeDtypeStruct(a.shape, F32) for a in (adj_e, adj_h, permittivity))
    results = pl.pallas_call(
        functools.partial(kernel, n),
        out_shape=tuple(pltpu.VMEM(a.shape, F32) for a in shapes),
        in_specs=[hbm] * 6 + [smem, hbm, smem],
        out_specs=(vmem, vmem, vmem),
        scratch_shapes=scratch,
        compiler_params=pltpu.CompilerParams(
            collective_id=0, has_side_effects=True, vmem_limit_bytes=60 * 1024 * 1024
        ),
    )(
        adj_e, adj_h, fwd_e, permittivity, design_mask, inverse, omega,
        port_mode.reshape(cells // LANES, LANES), port_plane,
    )
    return tuple(
        pl.pallas_call(
            write_out,
            out_shape=shapes,
            in_specs=[pl.BlockSpec(memory_space=pl.ANY)] * 3,
            out_specs=(hbm, hbm, hbm),
            scratch_shapes=[pltpu.SemaphoreType.DMA((7,))],
            compiler_params=pltpu.CompilerParams(vmem_limit_bytes=1024 * 1024),
        )(*results)
    )


def per_device(adj_e, adj_h, fwd_e, permittivity, design_mask, inverse, omega, port_mode, port_plane):
    args = (adj_e, adj_h, fwd_e, permittivity, design_mask, inverse, omega, port_mode, port_plane)
    paired = 2 * adj_e.shape[2] == LANES and fwd_e.shape[0] == 2 and lax.axis_size("exc") == 2 and permittivity.shape[0] == 1
    return fused(*args) if paired else plain_per_device(*args)


def solution(mesh):
    in_specs = (
        P(None, "exc", "line", None),
        P(None, "exc", "line", None),
        P(None, None, "exc", "line", None),
        P(None, "line", None),
        P(None, "line", None),
        P(),
        P("exc"),
        P("exc"),
        P("exc"),
    )
    out_specs = (P(None, "exc", "line", None), P(None, "exc", "line", None), P("exc", "line", None))
    return jax.shard_map(
        per_device, mesh=mesh, in_specs=in_specs, out_specs=out_specs, check_vma=False
    )
```

```python
import functools

import jax
import jax.numpy as jnp
from jax import lax
from jax.experimental import pallas as pl
from jax.experimental.pallas import tpu as pltpu
from jax.sharding import PartitionSpec as P

COURANT = 0.4


def extended(array, sides, width):
    for axis, dim in sides:
        devices, length = (lax.axis_size(axis), array.shape[dim])
        up = [(i, (i + 1) % devices) for i in range(devices - 1)]
        down = [(j, i) for i, j in up]
        last = lax.slice_in_dim(array, length - width, length, axis=dim)
        first = lax.slice_in_dim(array, 0, width, axis=dim)
        before = lax.ppermute(last, axis, up)
        after = lax.ppermute(first, axis, down)
        array = jnp.concatenate([before, array, after], axis=dim)
    return array


def lower_diff(padded, along):
    inner = padded.shape[along] - 2
    middle = lax.slice_in_dim(padded, 1, inner + 1, axis=along)
    return middle - lax.slice_in_dim(padded, 0, inner, axis=along)


def upper_diff(padded, along):
    inner = padded.shape[along] - 2
    middle = lax.slice_in_dim(padded, 1, inner + 1, axis=along)
    return lax.slice_in_dim(padded, 2, inner + 2, axis=along) - middle


def zero_rim(stacked, along):
    widths = [(0, 0)] * stacked.ndim
    widths[along] = (1, 1)
    return jnp.pad(stacked, widths)


def row_rim(stacked, along):
    return extended(stacked, (("line", 2),), 1)


def column_rim(stacked, along):
    return extended(stacked, (("line", 2),), 1)


def curl_along_y(fields, inverse_eps, extend, along):
    electric_x, electric_y, electric_z = (fields[0], fields[1], fields[2])
    magnetic_x, magnetic_y, magnetic_z = (fields[3], fields[4], fields[5])
    scaled = COURANT * inverse_eps
    lower_terms = lower_diff(extend(jnp.stack([magnetic_x, magnetic_z]), along), along)
    electric_x = electric_x + scaled * lower_terms[1]
    electric_z = electric_z - scaled * lower_terms[0]
    upper_terms = upper_diff(extend(jnp.stack([electric_x, electric_z]), along), along)
    magnetic_x = magnetic_x - COURANT * upper_terms[1]
    magnetic_z = magnetic_z + COURANT * upper_terms[0]
    return jnp.stack([electric_x, electric_y, electric_z, magnetic_x, magnetic_y, magnetic_z])


def curl_along_xz(fields, inverse_eps, extend, along):
    electric_x, electric_y, electric_z = (fields[0], fields[1], fields[2])
    magnetic_x, magnetic_y, magnetic_z = (fields[3], fields[4], fields[5])
    scaled = COURANT * inverse_eps
    depth_terms = lower_diff(zero_rim(jnp.stack([magnetic_x, magnetic_y]), 1), 1)
    across = lower_diff(extend(jnp.stack([magnetic_y, magnetic_z]), along), along)
    electric_x = electric_x - scaled * depth_terms[1]
    electric_y = electric_y + scaled * (depth_terms[0] - across[1])
    electric_z = electric_z + scaled * across[0]
    depth_upper = upper_diff(zero_rim(jnp.stack([electric_x, electric_y]), 1), 1)
    across_upper = upper_diff(extend(jnp.stack([electric_y, electric_z]), along), along)
    magnetic_x = magnetic_x + COURANT * depth_upper[1]
    magnetic_y = magnetic_y + COURANT * (across_upper[1] - depth_upper[0])
    magnetic_z = magnetic_z - COURANT * across_upper[0]
    return jnp.stack([electric_x, electric_y, electric_z, magnetic_x, magnetic_y, magnetic_z])


def line_solve(rounded, inverse):
    flattened = rounded.reshape(-1, rounded.shape[-1])
    solved = lax.dot_general(
        flattened, inverse, (((1,), (1,)), ((), ())), preferred_element_type=jnp.float32
    )
    return solved.reshape(rounded.shape)


def fold_lines(field, line_count):
    strip_width = field.shape[-2]
    block = field.shape[-1] // line_count
    regrouped = field.reshape(field.shape[:-2] + (strip_width, line_count, block))
    regrouped = jnp.moveaxis(regrouped, -3, -1)
    return regrouped.reshape(field.shape[:-2] + (line_count, block * strip_width))


def unfold(received, block):
    line_count = received.shape[-2]
    strip_width = received.shape[-1] // block
    regrouped = received.reshape(received.shape[:-2] + (line_count, block, strip_width))
    regrouped = jnp.moveaxis(regrouped, -3, -2)
    return regrouped.reshape(received.shape[:-2] + (block, line_count * strip_width))


def accumulate(gradient, fields, snapshot, mask_weight, inverse_cols):
    forward = snapshot.astype(jnp.float32)
    intersection = fields[0] * forward[0] + fields[1] * forward[1] + fields[2] * forward[2]
    return gradient + mask_weight * intersection * (inverse_cols * inverse_cols)


def plain_per_device(
    adj_e, adj_h, fwd_e, permittivity, design_mask, inverse, omega, port_mode, port_plane
):
    line_cells = inverse.shape[0]
    strip_width = adj_e.shape[2]
    step_count = fwd_e.shape[0]
    line_count = lax.axis_size("line")
    fields = jnp.concatenate([adj_e, adj_h], 0)
    inverse_rows = 1.0 / permittivity
    eps_turned = lax.all_to_all(
        fold_lines(permittivity, line_count), "line", split_axis=1, concat_axis=1, tiled=True
    )
    inverse_cols = 1.0 / unfold(eps_turned, strip_width)
    frequency = omega[0]
    plane_at = port_plane[0]
    offset = lax.axis_index("line") * strip_width
    column = (jnp.arange(line_cells, dtype=jnp.int32) == plane_at).astype(jnp.float32)
    profile_rows = lax.dynamic_slice_in_dim(port_mode, offset, strip_width)
    mask_weight = design_mask.astype(jnp.float32)
    gradient = jnp.zeros(permittivity.shape, jnp.float32)
    for instant in range(step_count):
        amplitude = jnp.cos(frequency * (instant + 1))
        fields = fields.at[2].add(amplitude * profile_rows[None, :, None] * column[None, None, :])
        fields = curl_along_y(fields, inverse_rows, row_rim, 2)
        fields = line_solve(fields.astype(jnp.bfloat16), inverse)
        turned = unfold(
            lax.all_to_all(
                fold_lines(fields, line_count), "line", split_axis=2, concat_axis=2, tiled=True
            ),
            strip_width,
        )
        turned = curl_along_xz(turned, inverse_cols, column_rim, 2)
        turned = line_solve(turned.astype(jnp.bfloat16), inverse)
        gradient = accumulate(gradient, turned, fwd_e[instant], mask_weight, inverse_cols)
        if instant + 1 < step_count:
            fields = unfold(
                lax.all_to_all(
                    fold_lines(turned, line_count), "line", split_axis=2, concat_axis=2, tiled=True
                ),
                strip_width,
            )
    return (turned[:3], turned[3:], gradient)


LANES = 128
MESH = pl.DeviceIdType.MESH
PAD = 8
EDGE = 16
F32, BF16 = (jnp.float32, jnp.bfloat16)


def contract(left, right):
    return lax.dot_general(left, right, (((1,), (1,)), ((), ())), preferred_element_type=F32)


def shifted_down(value, first):
    row = lax.broadcasted_iota(jnp.int32, value.shape, 0)
    return jnp.where(row == 0, first, pltpu.roll(value, 1, 0))


def shifted_up(value, last):
    rows = value.shape[0]
    row = lax.broadcasted_iota(jnp.int32, value.shape, 0)
    return jnp.where(row == rows - 1, last, pltpu.roll(value, rows - 1, 0))


def kernel(
    n, e_hbm, h_hbm, fwd_hbm, perm_hbm, mask_hbm, inv_hbm, omega, mode_hbm, plane,
    oe, oh, og,
    e, h, fwd, perm, mask, inv, halo, halo_lo, halo_hi, p_send, p_recv, eps_t, r_first, r_second, inv_eps,
    mode_v, mode_col, lines, solved, kept, send, recv, send_two, recv_two, grad,
    load_sem, hand_sem, halo_send_sem, halo_recv_sem, p_send_sem, p_recv_sem, send_sem, recv_sem,
):
    me, core = (lax.axis_index("line"), lax.axis_index("exc"))
    strip = perm.shape[0]
    cells = perm.shape[1]
    half = strip // 4
    inverse = inv.at[EDGE : cells + EDGE]
    above, below = (lax.rem(me + 1, n), lax.rem(me + n - 1, n))

    barrier = pltpu.get_barrier_semaphore()

    turns = sorted(range(1, n), key=lambda k: -min(k, n - k))
    others = [lax.rem(me + k, n) for k in turns]
    for other in others:
        pl.semaphore_signal(barrier, inc=1, device_id={"line": other}, device_id_type=MESH)

    pl.semaphore_signal(barrier, inc=1, device_id={"exc": 1 - core}, device_id_type=MESH)

    loads = []
    for source, target in (
        (e_hbm.at[:, 0], e), (h_hbm.at[:, 0], h), (perm_hbm.at[0], perm), (mode_hbm, mode_v), (inv_hbm, inverse),
        (fwd_hbm.at[:, :, 0], fwd), (mask_hbm.at[0], mask),
    ):
        copy = pltpu.make_async_copy(source, target, load_sem.at[len(loads)])
        copy.start()
        loads.append(copy)

    lane = lax.broadcasted_iota(jnp.int32, (1, LANES), 1)
    low = lane < strip

    for load in loads[:3]:
        load.wait()
    halo[...] = jnp.concatenate(
        [
            e[0, 0:1, :], e[2, 0:1, :], h[0, 0:1, :], h[2, 0:1, :], perm[0:1, :],
            h[0, strip - 1 : strip, :], h[2, strip - 1 : strip, :], perm[0:1, :],
        ],
        0,
    )

    pl.semaphore_wait(barrier, n)

    to_above = pltpu.make_async_remote_copy(
        halo, halo_lo, halo_send_sem.at[0], halo_recv_sem.at[0], device_id={"line": above}, device_id_type=MESH
    )
    to_below = pltpu.make_async_remote_copy(
        halo, halo_hi, halo_send_sem.at[1], halo_recv_sem.at[1], device_id={"line": below}, device_id_type=MESH
    )
    to_above.start()
    to_below.start()

    twice = jnp.concatenate([perm[...], perm[...]], 0)
    eps_t[...] = twice.T
    for block in range(n):
        first = eps_t[block * strip : block * strip + strip // 2, :]
        second = eps_t[block * strip + strip // 2 : (block + 1) * strip, :]
        p_send[block] = jnp.where(low, first, second)
    def p_copy(to, slot):
        return pltpu.make_async_remote_copy(
            p_send.at[to, pl.ds(pl.multiple_of(core * half, half), half)], p_recv.at[core, slot], p_send_sem.at[to], p_recv_sem.at[slot],
            device_id={"line": to}, device_id_type=MESH,
        )

    for other in others:
        p_copy(other, me).start()
    p_recv[core, me] = p_send[me, pl.ds(pl.multiple_of(core * half, half), half), :]

    r_first[0:cells, :] = COURANT * (1.0 / eps_t[...])
    r_first[cells:, :] = jnp.zeros((PAD, LANES), F32)

    loads[3].wait()
    for block in range(cells // LANES):
        line = jnp.broadcast_to(mode_v[block : block + 1, :], (LANES, LANES))
        mode_col[block * LANES : (block + 1) * LANES, :] = line.T
    mode_col[cells:, :] = jnp.zeros((PAD, LANES), F32)
    amplitudes = [jnp.cos(jnp.full((1, LANES), omega[0] * (s + 1), F32)) for s in range(2)]
    at_plane = plane[0]

    is_first, is_last = (me == 0, me == n - 1)
    x_at = lax.broadcasted_iota(jnp.int32, (1, cells), 1)
    column = jnp.where(x_at == at_plane, 1.0, 0.0)
    profile = mode_col[pl.ds(pl.multiple_of(me * strip, strip), strip + PAD), :] * amplitudes[0]
    profile = jnp.concatenate([profile] * (cells // LANES), 1)
    source = profile * column
    r = COURANT * (1.0 / perm[...])
    ex, ez, hx, hz = (e[0], e[2] + source[0:strip], h[0], h[2])
    to_above.wait()
    to_below.wait()
    hx_lo = jnp.where(is_first, 0.0, halo_lo[5:6, :])
    hz_lo = jnp.where(is_first, 0.0, halo_lo[6:7, :])
    ex = ex + r * (hz - shifted_down(hz, hz_lo))
    ez = ez - r * (hx - shifted_down(hx, hx_lo))
    r_hi = COURANT * (1.0 / halo_hi[4:5, :])
    ex_hi = halo_hi[0:1, :] + r_hi * (halo_hi[3:4, :] - hz[strip - 1 : strip])
    ez_hi = halo_hi[1:2, :] + source[strip : strip + 1] - r_hi * (halo_hi[2:3, :] - hx[strip - 1 : strip])
    ex_hi = jnp.where(is_last, 0.0, ex_hi)
    ez_hi = jnp.where(is_last, 0.0, ez_hi)
    hx = hx - COURANT * (shifted_up(ez, ez_hi) - ez)
    hz = hz + COURANT * (shifted_up(ex, ex_hi) - ex)
    for at, value in enumerate((ex, ez, h[1], e[1], hz, hx)):
        lines[at * strip : (at + 1) * strip, :] = value.astype(BF16)

    groups = ((0, 2), (2, 1), (3, 1), (4, 1), (5, 1), (6, 1), (7, 1), (8, 1))

    def copy_out(group, to, slot):
        first, count = groups[group]
        if count == 2:
            out, into = (send_two.at[to], recv_two.at[slot])
        else:
            out, into = (send.at[first - 2, to], recv.at[first - 2, slot])
        return pltpu.make_async_remote_copy(
            out, into, send_sem.at[group, to], recv_sem.at[group, slot],
            device_id={"line": to}, device_id_type=MESH,
        )

    def tile_at(tile, one, two, device):
        return two.at[device, tile] if tile < 2 else one.at[tile - 2, device]

    def send_all(group):
        for other in others:
            copy_out(group, other, me).start()
        keep_own(group)

    def keep_own(group):
        first, count = groups[group]
        for tile in range(first, first + count):
            tile_at(tile, recv, recv_two, me)[...] = tile_at(tile, send, send_two, me)[...]

    def receive_all(group):
        def take(k, carry):
            other = lax.rem(me + k, n)
            copy_out(group, other, other).wait_recv()
            return carry

        lax.fori_loop(1, n, take, 0)

    def assemble(message, tile):
        at = tile * LANES
        for k in range(n // 2):
            a, b = [tile_at(message, recv, recv_two, 2 * k + odd)[...] for odd in range(2)]
            cut = slice(k * LANES, (k + 1) * LANES)
            lines[at : at + strip, cut] = jnp.concatenate([a[:, :strip], b[:, :strip]], 1)
            lines[at + strip : at + LANES, cut] = jnp.concatenate([a[:, strip:], b[:, strip:]], 1)

    def solve_tile(tile):
        part = lines[tile * LANES : (tile + 1) * LANES, :]
        solved[tile, PAD : cells + PAD, :] = contract(inverse[...], part)

    rows = LANES

    def put(message, device, tile):
        for part in range(rows // strip):
            target = tile_at(message, send, send_two, device + part)
            target[...] = tile[part * strip : (part + 1) * strip].astype(BF16)

    def swap(tile):
        return pltpu.roll(tile, LANES // 2, 1)

    def extended(tile, off, back):
        return solved[tile, off - back : off - back + rows + PAD, :]

    def next_row(value):
        return pltpu.roll(value, value.shape[0] - 1, 0)

    def in_grid(start):
        return lax.broadcasted_iota(jnp.int32, (rows + PAD, LANES), 0) + start < cells

    def curl_x_first(off, at, count):
        b, bd = (solved[1, off : off + count, :], solved[1, off - 1 : off - 1 + count, :])
        hy, hyd = (jnp.where(low, b, swap(b)), jnp.where(low, bd, swap(bd)))
        a = solved[0, off : off + count, :] + r_first[pl.ds(at, count), :] * jnp.where(low, -hy, hy - hyd)
        solved[0, off : off + count, :] = a
        return a

    def curl_x_second(off, at):
        a, b, c = (extended(0, off, 0), extended(1, off, 0), extended(2, off, 0))
        sa, sc = (swap(a), swap(c))
        dc = sc - swap(extended(2, off, 1))
        ey = b + r_first[pl.ds(at, rows + PAD), :] * (c - dc)
        ey = jnp.where(in_grid(at), ey, 0.0)
        hy = b + COURANT * ((next_row(sa) - sa) + a)
        sy = swap(ey)
        c = c - COURANT * jnp.where(low, next_row(sy) - sy, ey)
        return jnp.where(low, hy, ey)[0:rows], c[0:rows]

    def curl_y(tile, start, sign, source):
        t, td = (extended(tile, start + PAD, 0), extended(tile, start + PAD, 1))
        st, std = (swap(t), swap(td))
        p = t if source is None else t + source
        p = p + sign * r_second[start : start + rows + PAD, :] * (st - std)
        p = jnp.where(in_grid(start), p, 0.0)
        sp = swap(p)
        q = t + sign * COURANT * (next_row(sp) - sp)
        return jnp.where(low, p, q)[0:rows]

    def along(electric, instant):
        return (
            electric[0] * fwd[instant, 0].astype(F32)
            + electric[1] * fwd[instant, 1].astype(F32)
            + electric[2] * fwd[instant, 2].astype(F32)
        )

    starts = range(0, cells, rows)

    loads[4].wait()
    inv[0:EDGE, :] = jnp.zeros((EDGE, cells), BF16)
    inv[cells + EDGE :, :] = jnp.zeros((EDGE, cells), BF16)
    quarter, group = (cells // 4, n // 4)
    for turn in (2, 3, 1, 0):
        plane_of = lax.rem(me // group + turn, 4)
        at = pl.multiple_of(plane_of * quarter, quarter)
        result = contract(inv[pl.ds(at, quarter + 2 * EDGE), :], lines[...])
        for tile in range(3):
            solved[tile, 0 : quarter + 2 * EDGE, :] = result[:, tile * LANES : (tile + 1) * LANES]
        for part in range(0, quarter, rows):
            curl_x_first(EDGE + part, pl.multiple_of(at + part, rows), rows)
        curl_x_first(EDGE + quarter, pl.multiple_of(at + quarter, rows), PAD)
        for part in range(0, quarter, rows):
            b, c = curl_x_second(EDGE + part, pl.multiple_of(at + part, rows))
            a = solved[0, EDGE + part : EDGE + part + rows, :]
            device = plane_of * group + part // strip
            put(0, device, jnp.where(low, a, swap(c)))
            put(1, device, jnp.where(low, swap(a), c))
            put(2, device, b)
        for k in range(1 if turn == 0 else 0, group):
            other = plane_of * group + lax.rem(lax.rem(me, group) + k, group)
            copy_out(0, other, me).start()
    keep_own(0)
    send_all(1)

    for tile in range(3):
        solved[tile, 0:PAD, :] = jnp.zeros((PAD, LANES), F32)
        solved[tile, cells + PAD :, :] = jnp.zeros((PAD, LANES), F32)

    def p_take(k, carry):
        other = lax.rem(me + k, n)
        p_copy(other, other).wait_recv()
        return carry

    lax.fori_loop(1, n, p_take, 0)
    hand_over = pltpu.make_async_remote_copy(
        p_recv.at[core], p_recv.at[core], hand_sem.at[0], hand_sem.at[1],
        device_id={"exc": 1 - core}, device_id_type=MESH,
    )
    hand_over.start()
    hand_over.wait()
    for k in range(n // 2):
        cut = slice(k * LANES, (k + 1) * LANES)
        for part in range(2):
            a, b = (p_recv[part, 2 * k], p_recv[part, 2 * k + 1])
            one, two = (part * half, part * half + strip // 2)
            inv_eps[one : one + half, cut] = 1.0 / jnp.concatenate([a[:, :strip], b[:, :strip]], 1)
            inv_eps[two : two + half, cut] = 1.0 / jnp.concatenate([a[:, strip:], b[:, strip:]], 1)
    both = jnp.concatenate([inv_eps[...], inv_eps[...]], 0)
    r_second[0:cells, :] = COURANT * both.T
    r_second[cells:, :] = jnp.zeros((PAD, LANES), F32)
    loads[5].wait()
    loads[6].wait()

    receive_all(0)
    assemble(0, 0)
    solve_tile(0)
    for start in starts:
        kept[start : start + rows, :] = curl_y(0, start, 1.0, None)
    assemble(1, 1)
    solve_tile(1)
    here = jnp.where(low & (lane + me * strip == at_plane), 1.0, 0.0)
    for start in starts:
        source = (amplitudes[1] * mode_col[start : start + rows + PAD, :]) * here
        b = curl_y(1, start, -1.0, source)
        a = kept[start : start + rows, :]
        put(3, start // strip, jnp.where(low, a, swap(b)))
        put(5, start // strip, jnp.where(low, swap(a), b))
    send_all(2)
    receive_all(1)
    assemble(2, 2)
    solve_tile(2)
    for start in starts:
        put(4, start // strip, solved[2, start + PAD : start + PAD + rows, :])
    send_all(3)
    send_all(4)

    weight = mask[...].astype(F32)
    square = inv_eps[...] * inv_eps[...]
    electric = jnp.concatenate(
        [lines[0:strip, :], lines[LANES + strip * 0 : LANES + strip, :], lines[2 * LANES + strip :, :]], 0
    )
    electric = contract(electric, inverse[...])
    parts = (electric[0:strip], electric[2 * strip :], electric[strip : 2 * strip])
    grad[...] = weight * along(parts, 0) * square

    for tile in range(2):
        receive_all(2 + tile)
        assemble(3 + tile, tile)
        solve_tile(tile)
    for start in starts:
        put(6, start // strip, curl_x_first(start + PAD, start, rows))
    send_all(5)
    receive_all(4)
    assemble(5, 2)
    solve_tile(2)
    for start in starts:
        b, c = curl_x_second(start + PAD, start)
        put(7, start // strip, b)
        put(8, start // strip, c)
    send_all(6)
    send_all(7)

    receive_all(5)
    assemble(6, 0)
    pair = contract(lines[0:LANES, :], inverse[...])
    oe[0, 0] = pair[:strip]
    oe[2, 0] = pair[strip:]
    receive_all(6)
    assemble(7, 1)
    pair = contract(lines[LANES : 2 * LANES, :], inverse[...])
    oh[1, 0] = pair[:strip]
    oe[1, 0] = pair[strip:]
    og[0] = grad[...] + weight * along((oe[0, 0], pair[strip:], oe[2, 0]), 1) * square
    receive_all(7)
    assemble(8, 2)
    pair = contract(lines[2 * LANES :, :], inverse[...])
    oh[2, 0] = pair[:strip]
    oh[0, 0] = pair[strip:]

    def settle(k, carry):
        other = lax.rem(me + k, n)
        p_copy(other, other).wait_send()
        for group in range(len(groups)):
            copy_out(group, other, other).wait_send()
        return carry

    lax.fori_loop(1, n, settle, 0)


def write_out(e, h, g, oe, oh, og, sem):
    copies = []
    for source, target in ((e, oe), (h, oh)):
        for at in range(3):
            copies.append(pltpu.make_async_copy(source.at[at], target.at[at], sem.at[len(copies)]))
    copies.append(pltpu.make_async_copy(g, og, sem.at[len(copies)]))
    for copy in copies:
        copy.start()
    for copy in copies:
        copy.wait()


def fused(adj_e, adj_h, fwd_e, permittivity, design_mask, inverse, omega, port_mode, port_plane):
    n = lax.axis_size("line")
    cells, strip = (inverse.shape[0], adj_e.shape[2])
    steps = fwd_e.shape[0]
    hbm = pl.BlockSpec(memory_space=pltpu.HBM)
    vmem = pl.BlockSpec(memory_space=pltpu.VMEM)
    smem = pl.BlockSpec(memory_space=pltpu.SMEM)
    scratch = [
        pltpu.VMEM((3, strip, cells), F32),
        pltpu.VMEM((3, strip, cells), F32),
        pltpu.VMEM((steps, 3, strip, cells), BF16),
        pltpu.VMEM((strip, cells), F32),
        pltpu.VMEM((strip, cells), jnp.int32),
        pltpu.VMEM((cells + 2 * EDGE, cells), BF16),
        pltpu.VMEM((8, cells), F32),
        pltpu.VMEM((8, cells), F32),
        pltpu.VMEM((8, cells), F32),
        pltpu.VMEM((n, strip // 2, LANES), F32),
        pltpu.VMEM((2, n, strip // 4, LANES), F32),
        pltpu.VMEM((cells, LANES), F32),
        pltpu.VMEM((cells + PAD, LANES), F32),
        pltpu.VMEM((cells + PAD, LANES), F32),
        pltpu.VMEM((strip, cells), F32),
        pltpu.VMEM((cells // LANES, LANES), F32),
        pltpu.VMEM((cells + PAD, LANES), F32),
        pltpu.VMEM((6 * strip, cells), BF16),
        pltpu.VMEM((3, cells + 2 * PAD, LANES), F32),
        pltpu.VMEM((cells, LANES), F32),
        pltpu.VMEM((7, n, strip, LANES), BF16),
        pltpu.VMEM((7, n, strip, LANES), BF16),
        pltpu.VMEM((n, 2, strip, LANES), BF16),
        pltpu.VMEM((n, 2, strip, LANES), BF16),
        pltpu.VMEM((strip, cells), F32),
        pltpu.SemaphoreType.DMA((7,)),
        pltpu.SemaphoreType.DMA((2,)),
        pltpu.SemaphoreType.DMA((2,)),
        pltpu.SemaphoreType.DMA((2,)),
        pltpu.SemaphoreType.DMA((n,)),
        pltpu.SemaphoreType.DMA((n,)),
        pltpu.SemaphoreType.DMA((8, n)),
        pltpu.SemaphoreType.DMA((8, n)),
    ]
    shapes = tuple(jax.ShapeDtypeStruct(a.shape, F32) for a in (adj_e, adj_h, permittivity))
    results = pl.pallas_call(
        functools.partial(kernel, n),
        out_shape=tuple(pltpu.VMEM(a.shape, F32) for a in shapes),
        in_specs=[hbm] * 6 + [smem, hbm, smem],
        out_specs=(vmem, vmem, vmem),
        scratch_shapes=scratch,
        compiler_params=pltpu.CompilerParams(
            collective_id=0, has_side_effects=True, vmem_limit_bytes=60 * 1024 * 1024
        ),
    )(
        adj_e, adj_h, fwd_e, permittivity, design_mask, inverse, omega,
        port_mode.reshape(cells // LANES, LANES), port_plane,
    )
    return tuple(
        pl.pallas_call(
            write_out,
            out_shape=shapes,
            in_specs=[pl.BlockSpec(memory_space=pl.ANY)] * 3,
            out_specs=(hbm, hbm, hbm),
            scratch_shapes=[pltpu.SemaphoreType.DMA((7,))],
            compiler_params=pltpu.CompilerParams(vmem_limit_bytes=1024 * 1024),
        )(*results)
    )


def per_device(adj_e, adj_h, fwd_e, permittivity, design_mask, inverse, omega, port_mode, port_plane):
    args = (adj_e, adj_h, fwd_e, permittivity, design_mask, inverse, omega, port_mode, port_plane)
    paired = 2 * adj_e.shape[2] == LANES and fwd_e.shape[0] == 2 and lax.axis_size("exc") == 2 and permittivity.shape[0] == 1
    return fused(*args) if paired else plain_per_device(*args)


def solution(mesh):
    in_specs = (
        P(None, "exc", "line", None),
        P(None, "exc", "line", None),
        P(None, None, "exc", "line", None),
        P(None, "line", None),
        P(None, "line", None),
        P(),
        P("exc"),
        P("exc"),
        P("exc"),
    )
    out_specs = (P(None, "exc", "line", None), P(None, "exc", "line", None), P("exc", "line", None))
    return jax.shard_map(
        per_device, mesh=mesh, in_specs=in_specs, out_specs=out_specs, check_vma=False
    )
```
